32 devices in a mesh: groups: 2 (over y), shard: 2 (over x), expert: 4 (over z), section: 2 (over core).
Axes of the slice: x: 2, y: 2, z: 4, core: 2. Of those that a mesh axis runs over, the one named last changes fastest.
Arguments:
- tokens: bfloat16 [2, 512, 6144], P(None, ('groups', 'shard', 'expert')), parts along dimension 1, may hold values from -6 to 6
- norm_gain: float32 [2, 6144], P('section'), may hold values from 0.5 to 2
- route_ids: int32 [2, 2, 512, 2], P('section', None, ('groups', 'shard', 'expert')), parts along dimension 2, may hold values from 0 to 3, all different within a row; in each aligned block of 32 rows (0 to 31, 32 to 63, ..., all dimensions but the last counted through in order) at most 18 rows name the same one
- route_weights: float32 [2, 2, 512, 2], P('section', None, ('groups', 'shard', 'expert')), parts along dimension 2, may hold values from 0.25 to 1
- gate_blocks: bfloat16 [2, 4, 64, 1, 128, 128], P('section', 'expert', 'shard'), may hold values from -0.5 to 0.5
- up_blocks: bfloat16 [2, 4, 64, 1, 128, 128], P('section', 'expert', 'shard'), may hold values from -0.5 to 0.5
- down_blocks: bfloat16 [2, 4, 64, 1, 128, 128], P('section', 'expert', 'shard'), may hold values from -0.4375 to 0.4375
- gate_rows: int32 [2, 4, 64, 1], P('section', 'expert', 'shard'), may hold values from 0 to 47
- down_cols: int32 [2, 4, 64, 1], P('section', 'expert', 'shard'), may hold values from 0 to 47
Outputs:
- hidden_states: bfloat16 [2, 2, 512, 6144], P('section', None, ('groups', 'shard', 'expert')), parts along dimension 2
The draws below stay inside these ranges and needn't reach their ends.
There are 2 independent parts, one for each index of `groups`. The reference program is written for one: setup_inputs(seed, part) draws one part's arguments, and reference() takes and returns one part's arrays. A program takes and returns all parts, laid end to end along the dimension named above; an argument that names none is the same for every part. Nothing has to cross between parts.
Inputs may be any that keep to these rules, and one draw needn't show every extreme that they name: `route_ids`: the 2 experts of a token differ; among the 32 tokens of one device, one micro-batch and one layer, no expert is named by more than 18 tokens, a bound that some block reaches of them.
All inputs are finite; a program needn't handle non-finite values.
Results may differ from the reference program's by a relative error of at most 0.0064.
Values may be sent and summed in bfloat16 or wider, within the bound.
No kernel may reach another device: no remote copies, remote signals or barrier semaphores. Data moves between devices by JAX's collectives and lax.ppermute only.
A program may use at most 64 MiB of HBM per device.

```python
import math
import jax
import jax.numpy as jnp
import numpy as np
from jax import lax

D = 6144
FF = 8192
BLK = 128
KEEP = 1
TOP = 2
LAYERS = 2
MICRO = 2
TOK_MB = 32
EXPERTS = 4
CAP = 18
TOKENS = 256


def pick_blocks(key):
    block_rows = D // BLK
    scores = jax.random.randint(key, (LAYERS, EXPERTS, FF // BLK, block_rows), 0, 1 << 20, dtype=jnp.int32)
    scores = scores * block_rows + jnp.arange(block_rows, dtype=jnp.int32)
    return lax.top_k(scores, KEEP)[1].astype(jnp.int32)


def draw_gate_rows(key, part):
    return pick_blocks(jax.random.fold_in(key, 11))


def draw_down_cols(key, part):
    return pick_blocks(jax.random.fold_in(key, 23))


def block_scale(key, extent, pieces, smallest, high):
    factor_of, own = 1.0, jax.random.fold_in(key, 6)
    for position, shards_of in pieces:
        draws = jnp.exp(jax.random.uniform(jax.random.fold_in(own, position), (shards_of,), jnp.float32, smallest / len(pieces), high / len(pieces)))
        factor_of = factor_of * jnp.repeat(draws, extent[position] // shards_of).reshape([-1 if axis == position else 1 for axis in range(len(extent))])
    return factor_of


def assign_block(rng, own, number, rows, number_of, top, most, slope):
    order = jax.random.permutation(rng, number_of)
    packed, ordinary = load_shares(number_of, rows * top, most, slope, True), load_shares(number_of, rows * top, most, slope, False)
    places = jnp.arange(number_of)

    def named(lengths, offset_by):
        used = int((lengths > 0).sum())
        fixed = max(1, used // 4)
        shifted = fixed + (places - fixed + offset_by * (used - fixed)) % max(1, number_of - fixed)
        return jnp.zeros((number_of,), jnp.int32).at[order[jnp.where(places < fixed, places, shifted)]].set(jnp.asarray(lengths, jnp.int32))

    lengths = jnp.where(number % 4 == 0, named(packed, number // 4), named(ordinary, number - number // 4 - 1))
    mixed = jax.random.permutation(jax.random.fold_in(own, 3), number_of)
    donor, sink = mixed[0:number_of // 2 * 2:2], mixed[1:number_of // 2 * 2:2]
    room = jnp.minimum(lengths[donor] - 1, most - lengths[sink]) // 2
    room = jnp.where((donor == order[0]) | (sink == order[0]) | (lengths[sink] == 0), 0, jnp.maximum(room, 0))
    shifted = jax.random.randint(jax.random.fold_in(own, 4), (number_of // 2,), 0, 1 << 20) % (room + 1)
    lengths = lengths.at[donor].add(-shifted).at[sink].add(shifted)
    labels = jnp.searchsorted(jnp.cumsum(lengths), jnp.arange(rows * top), side="right").astype(jnp.int32)
    listing = labels.reshape(top, rows).T
    listing = listing[jax.random.permutation(jax.random.fold_in(own, 1), rows)]
    offset_by = jax.random.randint(jax.random.fold_in(own, 2), (rows, 1), 0, top)
    return jnp.take_along_axis(listing, (jnp.arange(top)[None, :] + offset_by) % top, axis=1)


def load_shares(count, total, reach, lean, full):
    weights = [(1 << 20) // math.isqrt(standing ** lean) + 1 for standing in range(1, count + 1)]
    largest = reach if full else min(reach, max(-(-total // count), total * weights[0] // sum(weights)))
    least = 1 if total - largest >= count - 1 else 0
    holding, rest = [largest] + [least] * (count - 1), total - largest - least * (count - 1)
    while rest > 0:
        free = [i for i in range(1, count) if holding[i] < largest] or [i for i in range(1, count) if holding[i] < reach]
        whole, remaining = sum([weights[i] for i in free]), rest
        for i in free:
            addition = min(reach - holding[i], max(1, remaining * weights[i] // whole), rest)
            holding[i] = holding[i] + addition
            rest = rest - addition
    return np.array(holding)


def gaussian(rng, shape, scale, most, pieces=(), held_as=jnp.bfloat16):
    array = jax.random.normal(rng, shape, jnp.float32) * scale
    if len(pieces) > 0:
        array = block_scale(rng, shape, pieces, -0.22, 0.18) * array
    return jnp.clip(array, min=-most, max=most).astype(held_as)


def setup_inputs(seed: int = 0, part: int = 0) -> dict:
    arg_keys = jax.random.split(jax.random.key(seed), 10)
    own_keys = jax.random.split(jax.random.fold_in(arg_keys[9], part), 10)
    tokens = gaussian(own_keys[0], (MICRO, TOKENS, D), 1.0, 6.0, ((1, 8),))
    norm_gain = jnp.clip(jnp.exp(math.log(2.0) - 1.3862944 * jax.random.uniform(arg_keys[1], (LAYERS, D), jnp.float32) ** block_scale(arg_keys[1], (LAYERS, D), ((0, 2),), -0.2, 0.2)), 0.5, 2.0)
    route_ids_keys = jax.random.split(jax.random.fold_in(own_keys[2], 1), LAYERS * MICRO * TOKENS // TOK_MB)
    route_ids_turns = jax.random.permutation(jax.random.fold_in(own_keys[2], 3), LAYERS * MICRO * TOKENS // TOK_MB)
    route_ids = jax.vmap(lambda own, number: assign_block(jax.random.fold_in(own_keys[2], 2), own, number, TOK_MB, EXPERTS, TOP, CAP, 2))(route_ids_keys, route_ids_turns).reshape((LAYERS, MICRO, TOKENS, TOP))
    route_weights = jnp.clip(0.25 + 0.75 * jax.random.uniform(own_keys[3], (LAYERS, MICRO, TOKENS, TOP), jnp.float32) ** block_scale(own_keys[3], (LAYERS, MICRO, TOKENS, TOP), ((0, 2), (2, 8)), -0.2, 0.2), 0.25, 1.0)
    gate_blocks = gaussian(arg_keys[4], (LAYERS, EXPERTS, FF // BLK, KEEP, BLK, BLK), (KEEP * BLK) ** -0.5, 0.5, ((0, 2), (1, 4), (2, 2)))
    up_blocks = gaussian(arg_keys[5], (LAYERS, EXPERTS, FF // BLK, KEEP, BLK, BLK), (KEEP * BLK) ** -0.5, 0.5, ((0, 2), (1, 4), (2, 2)))
    down_blocks = gaussian(arg_keys[6], (LAYERS, EXPERTS, FF // BLK, KEEP, BLK, BLK), (FF * KEEP * BLK // D) ** -0.5, 0.4375, ((0, 2), (1, 4), (2, 2)))
    gate_rows = draw_gate_rows(jax.random.fold_in(arg_keys[9], 71), part)
    down_cols = draw_down_cols(jax.random.fold_in(arg_keys[9], 71), part)
    return dict(tokens=tokens, norm_gain=norm_gain, route_ids=route_ids, route_weights=route_weights, gate_blocks=gate_blocks, up_blocks=up_blocks, down_blocks=down_blocks, gate_rows=gate_rows, down_cols=down_cols)


def normalize(values, gain_row):
    wide = values.astype(jnp.float32)
    scale = lax.rsqrt(lax.optimization_barrier(jnp.mean(wide * wide, axis=-1, keepdims=True)) + 1e-05)
    return (wide * scale * gain_row).astype(jnp.bfloat16)

def expert_rows(inputs, gate_w, up_w, down_w, row_index, col_index):
    row_total = inputs.shape[0]
    block_size = gate_w.shape[-1]
    block_rows = inputs.shape[1] // block_size
    blocks = inputs.reshape(row_total, block_rows, block_size)
    picked = jnp.take(blocks, row_index.reshape(-1), axis=1)
    picked = picked.reshape(row_total, row_index.shape[0], row_index.shape[1], block_size).astype(jnp.float32)
    gate = jnp.einsum('rckd,ckdf->rcf', picked, gate_w.astype(jnp.float32), precision=lax.Precision.HIGHEST)
    up_val = jnp.einsum('rckd,ckdf->rcf', picked, up_w.astype(jnp.float32), precision=lax.Precision.HIGHEST)
    hidden = (jax.nn.silu(gate) * up_val).astype(jnp.bfloat16).astype(jnp.float32)
    result = jnp.zeros((row_total, block_rows, block_size), jnp.float32)
    for kept in range(row_index.shape[1]):
        part_out = jnp.einsum('rcf,cfo->rco', hidden, down_w[:, kept].astype(jnp.float32), precision=lax.Precision.HIGHEST)
        result = result.at[:, col_index[:, kept].astype(jnp.int32)].add(part_out)
    return result.reshape(row_total, block_rows * block_size).astype(jnp.bfloat16)

def reference(tokens, norm_gain, route_ids, route_weights, gate_blocks, up_blocks, down_blocks, gate_rows, down_cols):
    limit = min(TOKENS, TOKENS // TOK_MB * CAP)
    state = tokens
    layer_outputs = []
    for layer in range(LAYERS):
        results = []
        for micro_index in range(MICRO):
            current = state[micro_index]
            normed = normalize(current, norm_gain[layer])
            chosen_ids = route_ids[layer, micro_index]
            chosen_weights = route_weights[layer, micro_index]
            total = current.astype(jnp.float32)
            for expert_index in range(EXPERTS):
                hits = chosen_ids == expert_index
                chosen = jnp.any(hits, axis=1)
                positions = jnp.nonzero(chosen, size=limit, fill_value=0)[0].astype(jnp.int32)
                valid = jnp.arange(limit, dtype=jnp.int32) < jnp.sum(chosen.astype(jnp.int32))
                weight_all = lax.optimization_barrier(jnp.sum(jnp.where(hits, chosen_weights, jnp.zeros((), chosen_weights.dtype)), axis=1))
                weight_rows = jnp.where(valid, weight_all[positions], jnp.zeros((), chosen_weights.dtype))
                produced = expert_rows(normed[positions], gate_blocks[layer, expert_index], up_blocks[layer, expert_index], down_blocks[layer, expert_index], gate_rows[layer, expert_index], down_cols[layer, expert_index])
                total = total.at[positions].add(weight_rows[:, None] * produced.astype(jnp.float32))
            results.append(total.astype(jnp.bfloat16))
        state = jnp.stack(results)
        layer_outputs.append(state)
    return jnp.stack(layer_outputs)
```

```python
import functools
import math

import jax
import jax.numpy as jnp
from jax import lax
from jax.experimental import pallas as pl
from jax.experimental.pallas import tpu as pltpu
from jax.sharding import PartitionSpec as P

TOP = 2
LANES = 128
EPS = 1e-05
MIB = 1 << 20


def up_to(value, unit):
    return -(-value // unit) * unit


def group_of(capacity):
    return 16 // math.gcd(capacity, 16)


def iota(shape, axis):
    return lax.broadcasted_iota(jnp.int32, shape, axis)


def split_by(values, unit):
    quotient = jnp.floor((values.astype(jnp.float32) + 0.5) * (1.0 / unit)).astype(jnp.int32)
    return quotient, values - quotient * unit


def dot(left, right, contract=((1,), (0,))):
    return lax.dot_general(left, right, (contract, ((), ())), preferred_element_type=jnp.float32)


def spread_columns(values, rows):
    tokens = values.shape[1]
    token = split_by(iota((rows, tokens), 0), tokens)[1]
    same = iota((rows, tokens), 1) == token
    return [
        jnp.sum(jnp.where(same, values[choice : choice + 1, :], 0.0), axis=1, keepdims=True) for choice in range(TOP)
    ]


def picks_to_send(ids, experts, capacity, group):
    tokens = ids.shape[1]
    expert = iota((up_to(experts, 16), tokens), 0)
    hit = (ids[0:1, :] == expert) | (ids[1:2, :] == expert)
    hit = jnp.where(hit, 1.0, 0.0).astype(jnp.bfloat16)
    shape = (tokens, group * tokens)
    block, token = split_by(iota(shape, 1), tokens)
    earlier = jnp.where(iota(shape, 0) < token, 1.0, 0.0).astype(jnp.bfloat16)
    same = jnp.where(iota(shape, 0) == token, 1.0, 0.0).astype(jnp.bfloat16)
    slot = dot(hit, earlier)
    here = dot(hit, same)
    first = (block[0:1, :] * capacity).astype(jnp.float32)
    key = jnp.where(here > 0.5, slot + first, -1.0)
    row = iota((group * capacity, group * tokens), 0).astype(jnp.float32)
    return jnp.concatenate(
        [jnp.where(row == key[k : k + 1, :], 1.0, 0.0) for k in range(experts)], axis=0
    ).astype(jnp.bfloat16)


def picks_to_mix(ids, experts, capacity, group):
    tokens = ids.shape[1]
    rows = group * tokens
    token = split_by(iota((rows, tokens), 0), tokens)[1]
    first = (split_by(iota((rows, 1), 0), tokens)[0] * capacity).astype(jnp.float32)
    columns = iota((rows, experts * group * capacity), 1).astype(jnp.float32)
    earlier = iota((rows, tokens), 1) < token
    chosen = spread_columns(ids.astype(jnp.float32), rows)
    parts = []
    for choice in range(TOP):
        expert = chosen[choice]
        named = (ids[0:1, :].astype(jnp.float32) == expert) | (ids[1:2, :].astype(jnp.float32) == expert)
        slot = jnp.sum(jnp.where(named & earlier, 1.0, 0.0), axis=1, keepdims=True)
        key = expert * (group * capacity) + first + slot
        parts.append(jnp.where(columns == key, 1.0, 0.0))
    return jnp.concatenate(parts, axis=0).astype(jnp.bfloat16)


class Layer:
    def __init__(self, info, layer, own, other):
        self.held = info[0] == layer
        self.section, self.own, self.other = info[0], own, other

    def rows(self, at):
        return jnp.where(self.held, self.own[at][0, self.section], self.other[at][0, self.section])

    def gain(self, at, block):
        lanes = slice(block * LANES, (block + 1) * LANES)
        return jnp.where(self.held, self.own[at][0:1, lanes], self.other[at][0:1, lanes])


def send_rows(ids, state, scale, gain_of, out, experts, group, capacity, tokens):
    count = group * capacity
    blocks = state.shape[0] // tokens
    picks = picks_to_send(ids, experts, capacity, group)
    scale = jnp.concatenate([scale] * group, axis=0)
    for number in range(blocks // group):
        rows = state[number * group * tokens : (number + 1) * group * tokens, :]
        gain = jnp.concatenate(
            [jnp.broadcast_to(gain_of(number * group + j), (tokens, LANES)) for j in range(group)], axis=0
        )
        normed = (rows.astype(jnp.float32) * scale * gain).astype(jnp.bfloat16)
        picked = dot(picks, normed).astype(jnp.bfloat16)
        for e in range(experts):
            start = e * blocks * capacity + number * count
            out[start : start + count, :] = picked[e * count : (e + 1) * count, :]


def first_send_kernel(experts, capacity, group, info, tokens_ref, ids, gain, other_ids, other_gain, *rest):
    out, given, state, arrived = rest[-4:]
    section = info[0]
    copy = pltpu.make_async_copy(tokens_ref.at[section], given, arrived.at[0])
    copy.start()
    copy.wait()
    layer = Layer(info, 0, (ids, gain), (other_ids, other_gain))
    tokens, width = given.shape
    blocks = width // LANES
    total = jnp.zeros((tokens, 1), jnp.float32)
    for b in range(blocks):
        part = given[:, b * LANES : (b + 1) * LANES]
        state[b * tokens : (b + 1) * tokens, :] = part
        wide = part.astype(jnp.float32)
        total += jnp.sum(wide * wide, axis=1, keepdims=True)
    scale = lax.rsqrt(total * (1.0 / width) + EPS)
    send_rows(layer.rows(0), state, scale, lambda b: layer.gain(1, b), out, experts, group, capacity, tokens)


def mix_rows(picks, base, weights, returned, number, experts, blocks, group, capacity, tokens):
    count = group * capacity
    starts = [e * blocks * capacity + number * count for e in range(experts)]
    given = jnp.concatenate([returned[start : start + count, :] for start in starts], axis=0)
    picked = dot(picks, given)
    rows = group * tokens
    total = base.astype(jnp.float32)
    for choice in range(TOP):
        total += weights[choice] * picked[choice * rows : (choice + 1) * rows, :]
    return total.astype(jnp.bfloat16)


def relay_kernel(experts, capacity, group, info, tokens_ref, returned, ids, weights, gain, other_ids, other_weights, other_gain, *rest):
    state_out, state, out, given, arrived = rest
    section = info[0]
    copy = pltpu.make_async_copy(tokens_ref.at[section], given, arrived.at[0])
    copy.start()
    first = Layer(info, 0, (ids, weights), (other_ids, other_weights))
    second = Layer(info, 1, (ids, gain), (other_ids, other_gain))
    tokens, width = given.shape
    blocks = width // LANES
    picks = picks_to_mix(first.rows(0), experts, capacity, group)
    shares = spread_columns(first.rows(1), group * tokens)
    total = jnp.zeros((tokens, 1), jnp.float32)
    copy.wait()
    for number in range(blocks // group):
        base = jnp.concatenate(
            [given[:, b * LANES : (b + 1) * LANES] for b in range(number * group, (number + 1) * group)], axis=0
        )
        mixed = mix_rows(picks, base, shares, returned, number, experts, blocks, group, capacity, tokens)
        state[number * group * tokens : (number + 1) * group * tokens, :] = mixed
        wide = mixed.astype(jnp.float32)
        square = jnp.sum(wide * wide, axis=1, keepdims=True)
        for j in range(group):
            b = number * group + j
            state_out[:, b * LANES : (b + 1) * LANES] = mixed[j * tokens : (j + 1) * tokens, :]
            total += square[j * tokens : (j + 1) * tokens, :]
    scale = lax.rsqrt(total * (1.0 / width) + EPS)
    send_rows(second.rows(0), state, scale, lambda b: second.gain(1, b), out, experts, group, capacity, tokens)


def last_kernel(experts, capacity, group, info, first, state, returned, ids, weights, other_ids, other_weights, out, leaving):
    layer = Layer(info, 1, (ids, weights), (other_ids, other_weights))
    tokens, width = out.shape
    blocks = width // LANES
    picks = picks_to_mix(layer.rows(0), experts, capacity, group)
    shares = spread_columns(layer.rows(1), group * tokens)
    for number in range(blocks // group):
        base = state[number * group * tokens : (number + 1) * group * tokens, :]
        mixed = mix_rows(picks, base, shares, returned, number, experts, blocks, group, capacity, tokens)
        for j in range(group):
            b = number * group + j
            out[:, b * LANES : (b + 1) * LANES] = mixed[j * tokens : (j + 1) * tokens, :]

    @pl.when(info[0] == 0)
    def _():
        leaving[...] = out[...]

    @pl.when(info[0] != 0)
    def _():
        leaving[...] = first[...]


def join_kernel(info, first, second, came, out):
    @pl.when(info[0] == 0)
    def _():
        out[0, 0] = first[...]
        out[0, 1] = came[...]

    @pl.when(info[0] != 0)
    def _():
        out[0, 0] = came[...]
        out[0, 1] = second[...]


def expert_kernel(section, experts, capacity, group, split, unroll, info, *refs):
    @pl.when(info[0] == section)
    def _():
        expert_rows(experts, capacity, group, split, unroll, *refs)


def expert_rows(experts, capacity, group, split, unroll, *refs):
    halves, first = [], 0
    for pieces in split:
        halves.append(refs[first : first + pieces])
        first += pieces
    given, out = refs[first], refs[-11]
    numbers, places, placed, weights, arrived, state, hidden, total, made, left = refs[-10:]
    blocks = state.shape[0]
    padded = state.shape[1] // experts
    columns = (weights.shape[1] - 1) // 3
    count = group * capacity
    sizes = [columns] * 3 + [1]

    def load(half, which):
        source, start = halves[half][0], which * columns
        if len(halves[half]) > 1:
            source, start = halves[half][min(which, 2)], columns if which == 3 else 0
        return pltpu.make_async_copy(
            source.at[pl.ds(start, sizes[which])],
            weights.at[half, pl.ds(which * columns, sizes[which])],
            arrived.at[half, which],
        )

    for which in (3, 0, 1, 2):
        for half in range(len(halves)):
            load(half, which).start()

    shape = (group * padded, count)
    block, slot = split_by(iota((group * padded, 1), 0), padded)
    key = jnp.where(slot < capacity, block * capacity + slot, -1)
    spread = jnp.where(iota(shape, 1) == key, 1.0, 0.0).astype(jnp.bfloat16)
    for number in range(blocks // group):
        starts = [e * blocks * capacity + number * count for e in range(experts)]
        spaced = [dot(spread, given[start : start + count, :]) for start in starts]
        for j in range(group):
            rows = jnp.concatenate([s[j * padded : (j + 1) * padded, :] for s in spaced], axis=0)
            state[number * group + j] = rows.astype(jnp.bfloat16)
            total[number * group + j] = jnp.zeros(rows.shape, jnp.float32)

    for half in range(len(halves)):
        load(half, 3).wait()
        numbers[half] = weights[half, 3 * columns, :16, :].astype(jnp.float32)[:8, :].astype(jnp.int32)
    moves = [pltpu.make_async_copy(numbers.at[half], places.at[half], placed.at[half]) for half in range(len(halves))]
    for move in moves:
        move.start()
    for move in moves:
        move.wait()

    for half in range(len(halves)):
        load(half, 0).wait()
        load(half, 1).wait()

        def up_step(at, carry, half=half):
            for i in range(unroll):
                c = at * unroll + i
                rows = state[places[half, 0, c]]
                both = dot(rows, jnp.concatenate([weights[half, c], weights[half, columns + c]], axis=1))
                gate, up = both[:, :LANES], both[:, LANES:]
                hidden[half * columns + c] = (gate / (1.0 + jnp.exp(-gate)) * up).astype(jnp.bfloat16)
            return carry

        lax.fori_loop(0, columns // unroll, up_step, 0)

    for half in range(len(halves)):
        load(half, 2).wait()

        def down_step(at, carry, half=half):
            produced = []
            for i in range(unroll):
                c = at * unroll + i
                produced.append(dot(hidden[half * columns + c], weights[half, 2 * columns + c]))
            for i in range(unroll):
                to = places[half, 1, at * unroll + i]
                total[to] = total[to] + produced[i]
            return carry

        lax.fori_loop(0, columns // unroll, down_step, 0)

    block, slot = split_by(iota((count, 1), 0), capacity)
    packing = jnp.where(iota((count, group * padded), 1) == block * padded + slot, 1.0, 0.0).astype(jnp.bfloat16)
    size = blocks * capacity
    copies = [
        pltpu.make_async_copy(made.at[pl.ds(e * size, size)], out.at[pl.ds(e * size, size)], left.at[e])
        for e in range(experts)
    ]
    for e in range(experts):
        for number in range(blocks // group):
            spaced = jnp.concatenate(
                [total[number * group + j, e * padded : (e + 1) * padded, :] for j in range(group)], axis=0
            ).astype(jnp.bfloat16)
            start = e * size + number * count
            made[start : start + count, :] = dot(packing, spaced).astype(jnp.bfloat16)
        copies[e].start()
    for copy in copies:
        copy.wait()


def pack_kernel(info, in_rows, out_cols, *refs):
    stored, (out, kept, arrived, left) = refs[:3], refs[-4:]
    columns = (kept.shape[0] - 1) // 3

    def take(which):
        return pltpu.make_async_copy(stored[which], kept.at[pl.ds(which * columns, columns)], arrived.at[which])

    def give(which):
        span = pl.ds(which * columns, columns + which // 2)
        return pltpu.make_async_copy(kept.at[span], out.at[span], left.at[which])

    for which in range(3):
        take(which).start()
    spread = jnp.where(iota((columns, LANES), 0) == iota((columns, LANES), 1), 1.0, 0.0).astype(jnp.bfloat16)
    row = iota((LANES, LANES), 0)
    rows, cols = (
        dot(jnp.broadcast_to(p[...].astype(jnp.float32), (LANES, columns)).astype(jnp.bfloat16), spread)
        for p in (in_rows, out_cols)
    )
    kept[3 * columns] = jnp.where(row == 0, rows, jnp.where(row == 1, cols, 0.0)).astype(jnp.bfloat16)
    for which in range(3):
        take(which).wait()
        give(which).start()
    for which in range(3):
        give(which).wait()


def tie_kernel(*refs):
    pass


SMEM = pl.BlockSpec(memory_space=pltpu.SMEM)
VMEM = pl.BlockSpec(memory_space=pltpu.VMEM)
ANY = pl.BlockSpec(memory_space=pl.ANY)


def cost(microseconds):
    return pl.CostEstimate(flops=0, bytes_accessed=int(microseconds * 3.69e6), transcendentals=0)


def held(*arrays):
    return [pltpu.with_memory_space_constraint(a, pltpu.HBM) for a in arrays]


def pack(info, places, weights, after):
    columns, *block = weights[0].shape
    shape = (3 * columns + 1, *block)
    return pl.pallas_call(
        pack_kernel,
        out_shape=pltpu.HBM(shape, jnp.bfloat16),
        in_specs=[SMEM, VMEM, VMEM] + [ANY] * (3 + len(after)),
        out_specs=ANY,
        scratch_shapes=[
            pltpu.VMEM(shape, jnp.bfloat16),
            pltpu.SemaphoreType.DMA((3,)),
            pltpu.SemaphoreType.DMA((3,)),
        ],
        compiler_params=pltpu.CompilerParams(vmem_limit_bytes=8 * MIB),
        cost_estimate=cost(4),
        name="pack",
    )(info, *places, *held(*weights), *after)


def tie(array, *others):
    return pl.pallas_call(
        tie_kernel,
        out_shape=pltpu.HBM(array.shape, array.dtype),
        in_specs=[ANY] * (1 + len(others)),
        out_specs=ANY,
        input_output_aliases={0: 0},
        cost_estimate=cost(0),
        name="tie",
    )(*held(array), *others)


def body(tokens, norm_gain, route_ids, route_weights, gate_blocks, up_blocks, down_blocks, gate_rows, down_cols):
    experts = lax.axis_size("expert")
    sections = lax.axis_size("section")
    shards = lax.axis_size("shard")
    micro_count, row_count, width = tokens.shape
    assert sections == micro_count == TOP and gate_blocks.shape[1] == 1
    blocks = width // LANES
    capacity = min(row_count, max(row_count * 9 // 16, row_count * TOP // experts + 2))
    group = group_of(capacity)
    packed_rows = experts * blocks * capacity
    padded = up_to(capacity, 8)
    bf16, f32 = jnp.bfloat16, jnp.float32
    info = lax.axis_index("section").astype(jnp.int32).reshape(1)
    weights = [a.reshape(a.shape[2:3] + a.shape[4:]) for a in (gate_blocks, up_blocks, down_blocks)]
    places = [a.reshape(1, -1) for a in (gate_rows, down_cols)]
    ids, shares = jnp.swapaxes(route_ids, 2, 3), jnp.swapaxes(route_weights, 2, 3)
    swap = [(0, 1), (1, 0)]

    def across(array, section):
        pairs = [(a * sections + section, b * sections + section) for a, b in swap]
        return lax.ppermute(array, ("shard", "section"), pairs)

    def other(array, pairs=swap):
        return lax.ppermute(array, "section", pairs)

    paired = shards == 2
    if not paired:
        weights = [lax.all_gather(a, "shard", axis=0, tiled=True) for a in weights]
        places = [lax.all_gather(a, "shard", axis=1, tiled=True) for a in places]
    columns = weights[0].shape[0]
    assert columns <= LANES

    other_ids, other_shares, other_gain = other(ids), other(shares), other(norm_gain)
    rows_shape = jax.ShapeDtypeStruct((packed_rows, LANES), bf16)
    state_shape = jax.ShapeDtypeStruct((row_count, width), bf16)
    blocks_shape = jax.ShapeDtypeStruct((blocks * row_count, LANES), bf16)
    tokens_scratch = [pltpu.VMEM((row_count, width), bf16)]

    def call(kernel, name, microseconds, out_shape, args, specs, scratch, limit):
        return pl.pallas_call(
            kernel,
            out_shape=out_shape,
            in_specs=specs,
            out_specs=jax.tree.map(lambda _: VMEM, out_shape),
            scratch_shapes=scratch,
            compiler_params=pltpu.CompilerParams(vmem_limit_bytes=limit * MIB),
            cost_estimate=cost(microseconds),
            name=name,
        )(*args)

    def exchange(rows):
        rows = rows.reshape(experts, packed_rows // experts, LANES)
        return lax.all_to_all(rows, "expert", split_axis=0, concat_axis=0, tiled=True).reshape(packed_rows, LANES)

    def expert_on(section, sources, rows, earlier):
        return pl.pallas_call(
            functools.partial(
                expert_kernel, section, experts, capacity, group, [len(s) for s in sources], math.gcd(columns, 16)
            ),
            out_shape=rows_shape,
            in_specs=[SMEM] + [ANY] * sum(len(s) for s in sources) + [VMEM] + [ANY] * len(earlier),
            out_specs=ANY,
            scratch_shapes=[
                pltpu.VMEM((len(sources), 8, LANES), jnp.int32),
                pltpu.SMEM((len(sources), 8, LANES), jnp.int32),
                pltpu.SemaphoreType.DMA((len(sources),)),
                pltpu.VMEM((len(sources), 3 * columns + 1) + weights[0].shape[1:], bf16),
                pltpu.SemaphoreType.DMA((len(sources), 4)),
                pltpu.VMEM((blocks, experts * padded, LANES), bf16),
                pltpu.VMEM((len(sources) * columns, experts * padded, LANES), bf16),
                pltpu.VMEM((blocks, experts * padded, LANES), f32),
                pltpu.VMEM((packed_rows, LANES), bf16),
                pltpu.SemaphoreType.DMA((experts,)),
            ],
            input_output_aliases={2 + sum(len(s) for s in sources): 0} if earlier else {},
            compiler_params=pltpu.CompilerParams(vmem_limit_bytes=20 * MIB),
            cost_estimate=cost(7),
            name="expert",
        )(info, *held(*(a for s in sources for a in s)), rows, *earlier)

    packed = pack(info, places, weights, [])
    swapped = other(packed)
    sent = call(
        functools.partial(first_send_kernel, experts, capacity, group),
        "first_send",
        3,
        rows_shape,
        (info, *held(tokens), ids, norm_gain, other_ids, other_gain, packed, other_shares),
        [SMEM, ANY, VMEM, VMEM, VMEM, VMEM, ANY, ANY],
        tokens_scratch + [pltpu.VMEM((blocks * row_count, LANES), bf16), pltpu.SemaphoreType.DMA((1,))],
        12,
    )
    given_rows = exchange(sent)
    if paired:
        moved = tie(across(packed, 0), given_rows)
        passed = other(moved, [(0, 1)])
        sources = [[[packed], [moved]], [[swapped], [passed]]]
    else:
        sources = [[[packed]], [[swapped]]]
    done = expert_on(0, sources[0], given_rows, [])
    if paired:
        swapped = tie(swapped, done)
        whole = across(swapped, 0)
    returned = exchange(expert_on(1, sources[1], given_rows, [done]))
    first, state, sent = call(
        functools.partial(relay_kernel, experts, capacity, group),
        "relay",
        3,
        [state_shape, blocks_shape, rows_shape],
        (info, *held(tokens), returned, ids, shares, norm_gain, other_ids, other_shares, other_gain),
        [SMEM, ANY] + [VMEM] * 7,
        tokens_scratch + [pltpu.SemaphoreType.DMA((1,))],
        12,
    )
    given_rows = exchange(sent)
    if paired:
        whole = tie(whole, first)
        passed = other(whole, [(0, 1)])
        sources = [[[swapped], [whole]], [[packed], [passed]]]
    else:
        sources = [[[swapped]], [[packed]]]
    done = expert_on(0, sources[0], given_rows, [])
    returned = exchange(expert_on(1, sources[1], given_rows, [done]))
    second, leaving = call(
        functools.partial(last_kernel, experts, capacity, group),
        "last",
        3,
        [state_shape] * 2,
        (info, first, state, returned, ids, shares, other_ids, other_shares),
        [SMEM] + [VMEM] * 7,
        [],
        12,
    )
    return call(
        join_kernel,
        "join",
        1,
        jax.ShapeDtypeStruct((1, micro_count, row_count, width), bf16),
        (info, first, second, other(leaving)),
        [SMEM] + [VMEM] * 3,
        [],
        12,
    )


def solution(mesh):
    in_specs = (
        P(None, ("groups", "shard", "expert"), None),
        P("section", None),
        P("section", None, ("groups", "shard", "expert"), None),
        P("section", None, ("groups", "shard", "expert"), None),
        P("section", "expert", "shard", None, None, None),
        P("section", "expert", "shard", None, None, None),
        P("section", "expert", "shard", None, None, None),
        P("section", "expert", "shard", None),
        P("section", "expert", "shard", None),
    )
    out_specs = P("section", None, ("groups", "shard", "expert"), None)
    return jax.shard_map(body, mesh=mesh, in_specs=in_specs, out_specs=out_specs, check_vma=False)
```

```python
import functools
import itertools
import math

import jax
import jax.numpy as jnp
from jax import lax
from jax.experimental import pallas as pl
from jax.experimental.pallas import tpu as pltpu
from jax.sharding import PartitionSpec as P

TOP = 2
LANES = 128
EPS = 1e-05
MIB = 1 << 20


def up_to(value, unit):
    return -(-value // unit) * unit


def group_of(capacity):
    return 16 // math.gcd(capacity, 16)


def iota(shape, axis):
    return lax.broadcasted_iota(jnp.int32, shape, axis)


def split_by(values, unit):
    quotient = jnp.floor((values.astype(jnp.float32) + 0.5) * (1.0 / unit)).astype(jnp.int32)
    return quotient, values - quotient * unit


def dot(left, right, contract=((1,), (0,))):
    return lax.dot_general(left, right, (contract, ((), ())), preferred_element_type=jnp.float32)


def spread_columns(values, rows):
    tokens = values.shape[1]
    token = split_by(iota((rows, tokens), 0), tokens)[1]
    same = iota((rows, tokens), 1) == token
    return [
        jnp.sum(jnp.where(same, values[choice : choice + 1, :], 0.0), axis=1, keepdims=True) for choice in range(TOP)
    ]


def picks_to_send(ids, experts, capacity, group):
    tokens = ids.shape[1]
    expert = iota((up_to(experts, 16), tokens), 0)
    hit = (ids[0:1, :] == expert) | (ids[1:2, :] == expert)
    hit = jnp.where(hit, 1.0, 0.0).astype(jnp.bfloat16)
    shape = (tokens, group * tokens)
    block, token = split_by(iota(shape, 1), tokens)
    earlier = jnp.where(iota(shape, 0) < token, 1.0, 0.0).astype(jnp.bfloat16)
    same = jnp.where(iota(shape, 0) == token, 1.0, 0.0).astype(jnp.bfloat16)
    slot = dot(hit, earlier)
    here = dot(hit, same)
    first = (block[0:1, :] * capacity).astype(jnp.float32)
    key = jnp.where(here > 0.5, slot + first, -1.0)
    row = iota((group * capacity, group * tokens), 0).astype(jnp.float32)
    return jnp.concatenate(
        [jnp.where(row == key[k : k + 1, :], 1.0, 0.0) for k in range(experts)], axis=0
    ).astype(jnp.bfloat16)


def picks_to_mix(ids, experts, capacity, group):
    tokens = ids.shape[1]
    rows = group * tokens
    token = split_by(iota((rows, tokens), 0), tokens)[1]
    first = (split_by(iota((rows, 1), 0), tokens)[0] * capacity).astype(jnp.float32)
    columns = iota((rows, experts * group * capacity), 1).astype(jnp.float32)
    earlier = iota((rows, tokens), 1) < token
    chosen = spread_columns(ids.astype(jnp.float32), rows)
    parts = []
    for choice in range(TOP):
        expert = chosen[choice]
        named = (ids[0:1, :].astype(jnp.float32) == expert) | (ids[1:2, :].astype(jnp.float32) == expert)
        slot = jnp.sum(jnp.where(named & earlier, 1.0, 0.0), axis=1, keepdims=True)
        key = expert * (group * capacity) + first + slot
        parts.append(jnp.where(columns == key, 1.0, 0.0))
    return jnp.concatenate(parts, axis=0).astype(jnp.bfloat16)


class Layer:
    def __init__(self, info, layer, own, other):
        self.held = info[0] == layer
        self.section, self.me, self.own, self.other = info[0], info[1], own, other

    def rows(self, at):
        return jnp.where(self.held, self.own[at][0, self.section], self.other[at][0, self.section])

    def partners(self, at):
        return self.rows(at) ^ self.me

    def gain(self, at, block):
        lanes = slice(block * LANES, (block + 1) * LANES)
        return jnp.where(self.held, self.own[at][0:1, lanes], self.other[at][0:1, lanes])


def send_rows(partners, state, scale, gain_of, outs, group, capacity, tokens):
    count = group * capacity
    blocks = state.shape[0] // tokens
    picks = picks_to_send(partners, len(outs), capacity, group)
    scale = jnp.concatenate([scale] * group, axis=0)
    for number in range(blocks // group):
        rows = state[number * group * tokens : (number + 1) * group * tokens, :]
        gain = jnp.concatenate(
            [jnp.broadcast_to(gain_of(number * group + j), (tokens, LANES)) for j in range(group)], axis=0
        )
        normed = (rows.astype(jnp.float32) * scale * gain).astype(jnp.bfloat16)
        picked = dot(picks, normed).astype(jnp.bfloat16)
        for k, out in enumerate(outs):
            out[number * count : (number + 1) * count, :] = picked[k * count : (k + 1) * count, :]


def first_send_kernel(partners, capacity, group, info, tokens_ref, ids, gain, other_ids, other_gain, *rest):
    outs, (given, state, arrived) = rest[-partners - 3 : -3], rest[-3:]
    section = info[0]
    copy = pltpu.make_async_copy(tokens_ref.at[section], given, arrived.at[0])
    copy.start()
    copy.wait()
    layer = Layer(info, 0, (ids, gain), (other_ids, other_gain))
    tokens, width = given.shape
    blocks = width // LANES
    total = jnp.zeros((tokens, 1), jnp.float32)
    for b in range(blocks):
        part = given[:, b * LANES : (b + 1) * LANES]
        state[b * tokens : (b + 1) * tokens, :] = part
        wide = part.astype(jnp.float32)
        total += jnp.sum(wide * wide, axis=1, keepdims=True)
    scale = lax.rsqrt(total * (1.0 / width) + EPS)
    send_rows(layer.partners(0), state, scale, lambda b: layer.gain(1, b), outs, group, capacity, tokens)


def mix_rows(picks, base, weights, returned, number, group, capacity, tokens):
    count = group * capacity
    given = jnp.concatenate([part[number * count : (number + 1) * count, :] for part in returned], axis=0)
    picked = dot(picks, given)
    rows = group * tokens
    total = base.astype(jnp.float32)
    for choice in range(TOP):
        total += weights[choice] * picked[choice * rows : (choice + 1) * rows, :]
    return total.astype(jnp.bfloat16)


def relay_kernel(partners, capacity, group, info, tokens_ref, ids, weights, gain, other_ids, other_weights, other_gain, *rest):
    returned, (state_out, state), outs = rest[:partners], rest[-partners - 4 : -partners - 2], rest[-partners - 2 : -2]
    given, arrived = rest[-2:]
    section = info[0]
    copy = pltpu.make_async_copy(tokens_ref.at[section], given, arrived.at[0])
    copy.start()
    first = Layer(info, 0, (ids, weights), (other_ids, other_weights))
    second = Layer(info, 1, (ids, gain), (other_ids, other_gain))
    tokens, width = given.shape
    blocks = width // LANES
    picks = picks_to_mix(first.partners(0), partners, capacity, group)
    shares = spread_columns(first.rows(1), group * tokens)
    total = jnp.zeros((tokens, 1), jnp.float32)
    copy.wait()
    for number in range(blocks // group):
        base = jnp.concatenate(
            [given[:, b * LANES : (b + 1) * LANES] for b in range(number * group, (number + 1) * group)], axis=0
        )
        mixed = mix_rows(picks, base, shares, returned, number, group, capacity, tokens)
        state[number * group * tokens : (number + 1) * group * tokens, :] = mixed
        wide = mixed.astype(jnp.float32)
        square = jnp.sum(wide * wide, axis=1, keepdims=True)
        for j in range(group):
            b = number * group + j
            state_out[:, b * LANES : (b + 1) * LANES] = mixed[j * tokens : (j + 1) * tokens, :]
            total += square[j * tokens : (j + 1) * tokens, :]
    scale = lax.rsqrt(total * (1.0 / width) + EPS)
    send_rows(second.partners(0), state, scale, lambda b: second.gain(1, b), outs, group, capacity, tokens)


def last_kernel(partners, capacity, group, info, first, state, ids, weights, other_ids, other_weights, *rest):
    returned, (out, leaving) = rest[:partners], rest[partners:]
    layer = Layer(info, 1, (ids, weights), (other_ids, other_weights))
    tokens, width = out.shape
    blocks = width // LANES
    picks = picks_to_mix(layer.partners(0), partners, capacity, group)
    shares = spread_columns(layer.rows(1), group * tokens)
    for number in range(blocks // group):
        base = state[number * group * tokens : (number + 1) * group * tokens, :]
        mixed = mix_rows(picks, base, shares, returned, number, group, capacity, tokens)
        for j in range(group):
            b = number * group + j
            out[:, b * LANES : (b + 1) * LANES] = mixed[j * tokens : (j + 1) * tokens, :]

    @pl.when(info[0] == 0)
    def _():
        leaving[...] = out[...]

    @pl.when(info[0] != 0)
    def _():
        leaving[...] = first[...]


def join_kernel(info, first, second, came, out):
    @pl.when(info[0] == 0)
    def _():
        out[0, 0] = first[...]
        out[0, 1] = came[...]

    @pl.when(info[0] != 0)
    def _():
        out[0, 0] = came[...]
        out[0, 1] = second[...]


def expert_kernel(section, partners, capacity, group, split, unroll, info, *refs):
    @pl.when(info[0] == section)
    def _():
        expert_rows(partners, capacity, group, split, unroll, *refs)


def expert_rows(partners, capacity, group, split, unroll, *refs):
    halves, first = [], 0
    for pieces in split:
        halves.append(refs[first : first + pieces])
        first += pieces
    sent, outs = refs[first : -10 - partners][:partners], refs[-10 - partners : -10]
    numbers, places, placed, weights, arrived, state, hidden, total, made, left = refs[-10:]
    blocks = state.shape[0]
    padded = state.shape[1] // partners
    columns = (weights.shape[1] - 1) // 3
    count = group * capacity
    sizes = [columns] * 3 + [1]

    def part_of(k, number):
        return sent[k][number * count : (number + 1) * count, :]

    def load(half, which):
        source, start = halves[half][0], which * columns
        if len(halves[half]) > 1:
            source, start = halves[half][min(which, 2)], columns if which == 3 else 0
        return pltpu.make_async_copy(
            source.at[pl.ds(start, sizes[which])],
            weights.at[half, pl.ds(which * columns, sizes[which])],
            arrived.at[half, which],
        )

    for which in (3, 0, 1, 2):
        for half in range(len(halves)):
            load(half, which).start()

    shape = (group * padded, count)
    block, slot = split_by(iota((group * padded, 1), 0), padded)
    key = jnp.where(slot < capacity, block * capacity + slot, -1)
    spread = jnp.where(iota(shape, 1) == key, 1.0, 0.0).astype(jnp.bfloat16)
    for number in range(blocks // group):
        spaced = [dot(spread, part_of(k, number)) for k in range(partners)]
        for j in range(group):
            rows = jnp.concatenate([s[j * padded : (j + 1) * padded, :] for s in spaced], axis=0)
            state[number * group + j] = rows.astype(jnp.bfloat16)
            total[number * group + j] = jnp.zeros(rows.shape, jnp.float32)

    for half in range(len(halves)):
        load(half, 3).wait()
        numbers[half] = weights[half, 3 * columns, :16, :].astype(jnp.float32)[:8, :].astype(jnp.int32)
    moves = [pltpu.make_async_copy(numbers.at[half], places.at[half], placed.at[half]) for half in range(len(halves))]
    for move in moves:
        move.start()
    for move in moves:
        move.wait()

    for half in range(len(halves)):
        load(half, 0).wait()
        load(half, 1).wait()

        def up_step(at, carry, half=half):
            for i in range(unroll):
                c = at * unroll + i
                rows = state[places[half, 0, c]]
                both = dot(rows, jnp.concatenate([weights[half, c], weights[half, columns + c]], axis=1))
                gate, up = both[:, :LANES], both[:, LANES:]
                hidden[half * columns + c] = (gate / (1.0 + jnp.exp(-gate)) * up).astype(jnp.bfloat16)
            return carry

        lax.fori_loop(0, columns // unroll, up_step, 0)

    for half in range(len(halves)):
        load(half, 2).wait()

        def down_step(at, carry, half=half):
            produced = []
            for i in range(unroll):
                c = at * unroll + i
                produced.append(dot(hidden[half * columns + c], weights[half, 2 * columns + c]))
            for i in range(unroll):
                to = places[half, 1, at * unroll + i]
                total[to] = total[to] + produced[i]
            return carry

        lax.fori_loop(0, columns // unroll, down_step, 0)

    block, slot = split_by(iota((count, 1), 0), capacity)
    packing = jnp.where(iota((count, group * padded), 1) == block * padded + slot, 1.0, 0.0).astype(jnp.bfloat16)
    copies = [pltpu.make_async_copy(made.at[k], outs[k], left.at[k]) for k in range(partners)]
    for k in range(partners - 1, -1, -1):
        for number in range(blocks // group):
            spaced = jnp.concatenate(
                [total[number * group + j, k * padded : (k + 1) * padded, :] for j in range(group)], axis=0
            ).astype(jnp.bfloat16)
            made[k, number * count : (number + 1) * count, :] = dot(packing, spaced).astype(jnp.bfloat16)
        copies[k].start()
    for copy in copies:
        copy.wait()


def pack_kernel(info, in_rows, out_cols, *refs):
    stored, (out, kept, numbers, named, arrived, left) = refs[:3], refs[-6:]
    columns = stored[0].shape[0]
    names = [
        pltpu.make_async_copy(source, numbers.at[at], named.at[at]) for at, source in enumerate((in_rows, out_cols))
    ]

    def take(at):
        return pltpu.make_async_copy(stored[at], kept.at[pl.ds(at * columns, columns)], arrived.at[at])

    def give(at):
        span = pl.ds(at * columns, columns + at // 2)
        return pltpu.make_async_copy(kept.at[span], out.at[span], left.at[at])

    for name in names:
        name.start()
    for at in range(3):
        take(at).start()
    spread = jnp.where(iota((columns, LANES), 0) == iota((columns, LANES), 1), 1.0, 0.0).astype(jnp.bfloat16)
    row = iota((LANES, LANES), 0)
    for name in names:
        name.wait()
    rows, cols = (
        dot(jnp.broadcast_to(numbers[at].astype(jnp.float32), (LANES, columns)).astype(jnp.bfloat16), spread)
        for at in range(2)
    )
    kept[3 * columns] = jnp.where(row == 0, rows, jnp.where(row == 1, cols, 0.0)).astype(jnp.bfloat16)
    for at in range(3):
        take(at).wait()
        give(at).start()
    for at in range(3):
        give(at).wait()


def tie_kernel(*refs):
    pass


SMEM = pl.BlockSpec(memory_space=pltpu.SMEM)
VMEM = pl.BlockSpec(memory_space=pltpu.VMEM)
ANY = pl.BlockSpec(memory_space=pl.ANY)


def held(*arrays):
    return [pltpu.with_memory_space_constraint(a, pltpu.HBM) for a in arrays]


def pack(info, places, weights, after):
    columns, *block = weights[0].shape
    shape = (3 * columns + 1, *block)
    return pl.pallas_call(
        pack_kernel,
        out_shape=pltpu.HBM(shape, jnp.bfloat16),
        in_specs=[SMEM] + [ANY] * (5 + len(after)),
        out_specs=ANY,
        scratch_shapes=[
            pltpu.VMEM(shape, jnp.bfloat16),
            pltpu.VMEM((2, 1, columns), jnp.int32),
            pltpu.SemaphoreType.DMA((2,)),
            pltpu.SemaphoreType.DMA((3,)),
            pltpu.SemaphoreType.DMA((3,)),
        ],
        compiler_params=pltpu.CompilerParams(vmem_limit_bytes=8 * MIB),
        name="pack",
    )(info, *held(*places, *weights), *after)


def tie(array, *others):
    return pl.pallas_call(
        tie_kernel,
        out_shape=pltpu.HBM(array.shape, array.dtype),
        in_specs=[ANY] * (1 + len(others)),
        out_specs=ANY,
        input_output_aliases={0: 0},
        name="tie",
    )(*held(array), *others)


def body(tokens, norm_gain, route_ids, route_weights, gate_blocks, up_blocks, down_blocks, gate_rows, down_cols):
    partners = lax.axis_size("expert")
    sections = lax.axis_size("section")
    shards = lax.axis_size("shard")
    micro_count, row_count, width = tokens.shape
    assert sections == micro_count == 2 and gate_blocks.shape[1] == 1 and partners & (partners - 1) == 0
    blocks = width // LANES
    capacity = min(row_count, max(row_count * 9 // 16, row_count * TOP // partners + 2))
    group = group_of(capacity)
    rows_shape = jax.ShapeDtypeStruct((blocks * capacity, LANES), jnp.bfloat16)
    padded = up_to(capacity, 8)
    bf16, f32 = jnp.bfloat16, jnp.float32
    info = jnp.stack([lax.axis_index(a) for a in ("section", "expert", "groups")]).astype(jnp.int32)
    weights = [a.reshape(a.shape[2:3] + a.shape[4:]) for a in (gate_blocks, up_blocks, down_blocks)]
    places = [a.reshape(1, -1) for a in (gate_rows, down_cols)]
    ids, shares = jnp.swapaxes(route_ids, 2, 3), jnp.swapaxes(route_weights, 2, 3)
    swap = [(0, 1), (1, 0)]

    def across(array):
        axes = ("groups", "shard", "expert", "section")
        sizes = [lax.axis_size(a) for a in axes]
        pairs = []
        for place in itertools.product(*(range(n) for n in sizes)):
            target = list(place)
            turned = 0 if place[3] else 1
            target[turned] = 1 - place[turned]
            pairs.append(tuple(sum(p * math.prod(sizes[i + 1 :]) for i, p in enumerate(q)) for q in (place, target)))
        return lax.ppermute(array, axes, pairs)

    def other(array, pairs=swap):
        return lax.ppermute(array, "section", pairs)

    paired = shards == 2 and lax.axis_size("groups") == 2
    if not paired:
        weights = [lax.all_gather(a, "shard", axis=0, tiled=True) for a in weights]
        places = [lax.all_gather(a, "shard", axis=1, tiled=True) for a in places]
    columns = weights[0].shape[0]
    assert columns <= LANES

    other_ids, other_shares, other_gain = other(ids), other(shares), other(norm_gain)
    state_shape = jax.ShapeDtypeStruct((row_count, width), bf16)
    blocks_shape = jax.ShapeDtypeStruct((blocks * row_count, LANES), bf16)
    tokens_scratch = [pltpu.VMEM((row_count, width), bf16)]

    def call(kernel, name, out_shape, args, specs, scratch, limit):
        return pl.pallas_call(
            kernel,
            out_shape=out_shape,
            in_specs=specs,
            out_specs=jax.tree.map(lambda _: VMEM, out_shape),
            scratch_shapes=scratch,
            compiler_params=pltpu.CompilerParams(vmem_limit_bytes=limit * MIB),
            name=name,
        )(*args)

    def exchange(parts):
        moved = list(parts)
        for k in range(partners - 1, 0, -1):
            moved[k] = lax.ppermute(parts[k], "expert", [(i, i ^ k) for i in range(partners)])
        return moved

    def expert_on(section, sources, rows, earlier):
        inputs = sum(len(s) for s in sources)
        return pl.pallas_call(
            functools.partial(
                expert_kernel,
                section,
                partners,
                capacity,
                group,
                [len(s) for s in sources],
                math.gcd(columns, 16),
            ),
            out_shape=[pltpu.HBM(rows_shape.shape, bf16)] * partners,
            in_specs=[SMEM] + [ANY] * inputs + [VMEM] * len(rows) + [ANY] * len(earlier),
            out_specs=[ANY] * partners,
            scratch_shapes=[
                pltpu.VMEM((len(sources), 8, LANES), jnp.int32),
                pltpu.SMEM((len(sources), 8, LANES), jnp.int32),
                pltpu.SemaphoreType.DMA((len(sources),)),
                pltpu.VMEM((len(sources), 3 * columns + 1) + weights[0].shape[1:], bf16),
                pltpu.SemaphoreType.DMA((len(sources), 4)),
                pltpu.VMEM((blocks, partners * padded, LANES), bf16),
                pltpu.VMEM((len(sources) * columns, partners * padded, LANES), bf16),
                pltpu.VMEM((blocks, partners * padded, LANES), f32),
                pltpu.VMEM((partners,) + rows_shape.shape, bf16),
                pltpu.SemaphoreType.DMA((partners,)),
            ],
            input_output_aliases={1 + inputs + len(rows) + k: k for k in range(len(earlier))},
            compiler_params=pltpu.CompilerParams(vmem_limit_bytes=20 * MIB),
            name="expert",
        )(info, *(a for s in sources for a in s), *rows, *held(*earlier))

    packed = pack(info, places, weights, [])
    sent = call(
        functools.partial(first_send_kernel, partners, capacity, group),
        "first_send",
        [rows_shape] * partners,
        (info, *held(tokens), ids, norm_gain, other_ids, other_gain, other_shares),
        [SMEM, ANY, VMEM, VMEM, VMEM, VMEM, ANY],
        tokens_scratch + [pltpu.VMEM((blocks * row_count, LANES), bf16), pltpu.SemaphoreType.DMA((1,))],
        12,
    )
    rows = exchange(sent)
    swapped = other(pack(info, places, weights, rows[1:]))
    if paired:
        moved = tie(across(packed), *rows[1:])
        passed = other(moved, [(0, 1)])
        whole = across(swapped)
        sources = [[held(packed), held(moved)], [held(swapped), [passed]]]
    else:
        sources = [[held(packed)], [held(swapped)]]
    done = expert_on(0, sources[0], rows, [])
    returned = exchange(expert_on(1, sources[1], rows, done))
    first, state, *sent = call(
        functools.partial(relay_kernel, partners, capacity, group),
        "relay",
        [state_shape, blocks_shape] + [rows_shape] * partners,
        (info, *held(tokens), ids, shares, norm_gain, other_ids, other_shares, other_gain, *held(returned[0]), *returned[1:]),
        [SMEM, ANY] + [VMEM] * (6 + partners),
        tokens_scratch + [pltpu.SemaphoreType.DMA((1,))],
        12,
    )
    given_rows = exchange(sent)
    if paired:
        whole = tie(whole, first)
        passed = other(whole, [(0, 1)])
        sources = [[held(swapped), held(whole)], [held(packed), [passed]]]
    else:
        sources = [[held(swapped)], [held(packed)]]
    done = expert_on(0, sources[0], given_rows, [])
    returned = exchange(expert_on(1, sources[1], given_rows, done))
    second, leaving = call(
        functools.partial(last_kernel, partners, capacity, group),
        "last",
        [state_shape] * 2,
        (info, first, state, ids, shares, other_ids, other_shares, *held(returned[0]), *returned[1:]),
        [SMEM] + [VMEM] * (6 + partners),
        [],
        12,
    )
    return call(
        join_kernel,
        "join",
        jax.ShapeDtypeStruct((1, micro_count, row_count, width), bf16),
        (info, first, second, other(leaving)),
        [SMEM] + [VMEM] * 3,
        [],
        12,
    )


def solution(mesh):
    in_specs = (
        P(None, ("groups", "shard", "expert"), None),
        P("section", None),
        P("section", None, ("groups", "shard", "expert"), None),
        P("section", None, ("groups", "shard", "expert"), None),
        P("section", "expert", "shard", None, None, None),
        P("section", "expert", "shard", None, None, None),
        P("section", "expert", "shard", None, None, None),
        P("section", "expert", "shard", None),
        P("section", "expert", "shard", None),
    )
    out_specs = P("section", None, ("groups", "shard", "expert"), None)
    return jax.shard_map(body, mesh=mesh, in_specs=in_specs, out_specs=out_specs, check_vma=False)
```

```python
import functools
import itertools
import math

import jax
import jax.numpy as jnp
from jax import lax
from jax.experimental import pallas as pl
from jax.experimental.pallas import tpu as pltpu
from jax.sharding import PartitionSpec as P

TOP = 2
LANES = 128
EPS = 1e-05
MIB = 1 << 20


def up_to(value, unit):
    return -(-value // unit) * unit


def group_of(capacity):
    return 16 // math.gcd(capacity, 16)


def iota(shape, axis):
    return lax.broadcasted_iota(jnp.int32, shape, axis)


def split_by(values, unit):
    quotient = jnp.floor((values.astype(jnp.float32) + 0.5) * (1.0 / unit)).astype(jnp.int32)
    return quotient, values - quotient * unit


def dot(left, right, contract=((1,), (0,))):
    return lax.dot_general(left, right, (contract, ((), ())), preferred_element_type=jnp.float32)


def side_by_side(left, rights):
    products = []
    for at in range(0, len(rights), 2):
        pair = rights[at : at + 2]
        product = dot(left, jnp.concatenate(pair, axis=1))
        products += [product[:, i * LANES : (i + 1) * LANES] for i in range(len(pair))]
    return products


def spread_columns(values, rows):
    tokens = values.shape[1]
    token = split_by(iota((rows, tokens), 0), tokens)[1]
    same = iota((rows, tokens), 1) == token
    return [
        jnp.sum(jnp.where(same, values[choice : choice + 1, :], 0.0), axis=1, keepdims=True) for choice in range(TOP)
    ]


def picks_to_send(ids, experts, capacity, group):
    tokens = ids.shape[1]
    expert = iota((up_to(experts, 16), tokens), 0)
    hit = (ids[0:1, :] == expert) | (ids[1:2, :] == expert)
    hit = jnp.where(hit, 1.0, 0.0).astype(jnp.bfloat16)
    shape = (tokens, group * tokens)
    block, token = split_by(iota(shape, 1), tokens)
    earlier = jnp.where(iota(shape, 0) < token, 1.0, 0.0).astype(jnp.bfloat16)
    same = jnp.where(iota(shape, 0) == token, 1.0, 0.0).astype(jnp.bfloat16)
    slot = dot(hit, earlier)
    here = dot(hit, same)
    first = (block[0:1, :] * capacity).astype(jnp.float32)
    key = jnp.where(here > 0.5, slot + first, -1.0)
    row = iota((group * capacity, group * tokens), 0).astype(jnp.float32)
    return jnp.concatenate(
        [jnp.where(row == key[k : k + 1, :], 1.0, 0.0) for k in range(experts)], axis=0
    ).astype(jnp.bfloat16)


def picks_to_mix(ids, experts, capacity, group):
    tokens = ids.shape[1]
    rows = group * tokens
    token = split_by(iota((rows, tokens), 0), tokens)[1]
    first = (split_by(iota((rows, 1), 0), tokens)[0] * capacity).astype(jnp.float32)
    columns = iota((rows, experts * group * capacity), 1).astype(jnp.float32)
    earlier = iota((rows, tokens), 1) < token
    chosen = spread_columns(ids.astype(jnp.float32), rows)
    parts = []
    for choice in range(TOP):
        expert = chosen[choice]
        named = (ids[0:1, :].astype(jnp.float32) == expert) | (ids[1:2, :].astype(jnp.float32) == expert)
        slot = jnp.sum(jnp.where(named & earlier, 1.0, 0.0), axis=1, keepdims=True)
        key = expert * (group * capacity) + first + slot
        parts.append(jnp.where(columns == key, 1.0, 0.0))
    return jnp.concatenate(parts, axis=0).astype(jnp.bfloat16)


def send_rows(partners, state, scale, gain_of, outs, group, capacity, tokens):
    count = group * capacity
    blocks = state.shape[0] // tokens
    picks = picks_to_send(partners, len(outs), capacity, group)
    scale = jnp.concatenate([scale] * group, axis=0)
    normed = []
    for number in range(blocks // group):
        rows = state[number * group * tokens : (number + 1) * group * tokens, :]
        gain = jnp.concatenate(
            [jnp.broadcast_to(gain_of(number * group + j), (tokens, LANES)) for j in range(group)], axis=0
        )
        normed.append((rows.astype(jnp.float32) * scale * gain).astype(jnp.bfloat16))
    for number, picked in enumerate(side_by_side(picks, normed)):
        for k, out in enumerate(outs):
            out[number * count : (number + 1) * count, :] = picked[k * count : (k + 1) * count, :].astype(jnp.bfloat16)


def first_send_kernel(partners, capacity, group, info, tokens_ref, ids, gain, *rest):
    outs, (given, state, arrived) = rest[-partners - 3 : -3], rest[-3:]

    @pl.when(info[0] == 0)
    def _():
        copy = pltpu.make_async_copy(tokens_ref, given, arrived.at[0])
        copy.start()
        copy.wait()
        micro_count, tokens, width = given.shape
        blocks = width // LANES
        for micro in range(micro_count):
            total = jnp.zeros((tokens, 1), jnp.float32)
            for b in range(blocks):
                part = given[micro, :, b * LANES : (b + 1) * LANES]
                state[b * tokens : (b + 1) * tokens, :] = part
                wide = part.astype(jnp.float32)
                total += jnp.sum(wide * wide, axis=1, keepdims=True)
            scale = lax.rsqrt(total * (1.0 / width) + EPS)
            size = blocks * capacity
            targets = [out.at[micro * size : (micro + 1) * size, :] for out in outs]
            send_rows(ids[0, micro] ^ info[1], state, scale, lambda b: gain_of(gain, b), targets, group, capacity, tokens)


def gain_of(gain, block):
    return gain[0:1, block * LANES : (block + 1) * LANES]


def mix_rows(picks, base_of, weights, returned, blocks, group, capacity, tokens):
    count, rows = group * capacity, group * tokens
    given = [
        jnp.concatenate([part[number * count : (number + 1) * count, :] for part in returned], axis=0)
        for number in range(blocks // group)
    ]
    for number, picked in enumerate(side_by_side(picks, given)):
        total = base_of(number).astype(jnp.float32)
        for choice in range(TOP):
            total += weights[choice] * picked[choice * rows : (choice + 1) * rows, :]
        yield number, total.astype(jnp.bfloat16)


def relay_kernel(micro, partners, capacity, group, info, *refs):
    @pl.when(info[0] == 0)
    def _():
        relay_rows(micro, partners, capacity, group, info, *refs)


def relay_rows(micro, partners, capacity, group, info, tokens_ref, ids, weights, next_ids, next_gain, *rest):
    returned, (state_out, carry), outs = rest[:partners], rest[-partners - 3 : -partners - 1], rest[-partners - 1 : -2]
    given, arrived = rest[-2:]
    carried = carry.at[1]
    copy = pltpu.make_async_copy(tokens_ref.at[micro], given, arrived.at[0])
    copy.start()
    tokens, width = given.shape
    blocks = width // LANES
    state = carried.at[blocks * capacity : blocks * (capacity + tokens), :]
    picks = picks_to_mix(ids[0, micro] ^ info[1], partners, capacity, group)
    shares = spread_columns(weights[0, micro], group * tokens)
    total = jnp.zeros((tokens, 1), jnp.float32)
    copy.wait()

    def base_of(number):
        return jnp.concatenate(
            [given[:, b * LANES : (b + 1) * LANES] for b in range(number * group, (number + 1) * group)], axis=0
        )

    for number, mixed in mix_rows(picks, base_of, shares, returned, blocks, group, capacity, tokens):
        state[number * group * tokens : (number + 1) * group * tokens, :] = mixed
        wide = mixed.astype(jnp.float32)
        square = jnp.sum(wide * wide, axis=1, keepdims=True)
        for j in range(group):
            b = number * group + j
            state_out[:, b * LANES : (b + 1) * LANES] = mixed[j * tokens : (j + 1) * tokens, :]
            total += square[j * tokens : (j + 1) * tokens, :]
    scale = lax.rsqrt(total * (1.0 / width) + EPS)
    send_rows(
        next_ids[0, micro] ^ info[1], state, scale, lambda b: gain_of(next_gain, b), [carried, *outs], group, capacity, tokens
    )


def last_kernel(micro, partners, capacity, group, info, first, carried, ids, weights, *rest):
    returned, (out, made, done) = rest[:partners], rest[-3:]
    tokens, width = made.shape
    blocks = width // LANES
    keep = pltpu.make_async_copy(made, out.at[0, micro], done.at[0])

    @pl.when(info[0] == 0)
    def _():
        copy = pltpu.make_async_copy(first, made, done.at[1])
        copy.start()
        copy.wait()

    @pl.when(info[0] != 0)
    def _():
        picks = picks_to_mix(ids[0, micro] ^ info[1], partners, capacity, group)
        shares = spread_columns(weights[0, micro], group * tokens)

        def base_of(number):
            start = blocks * capacity + number * group * tokens
            return carried[start : start + group * tokens, :]

        for number, mixed in mix_rows(picks, base_of, shares, returned, blocks, group, capacity, tokens):
            for j in range(group):
                b = number * group + j
                made[:, b * LANES : (b + 1) * LANES] = mixed[j * tokens : (j + 1) * tokens, :]

    keep.start()
    keep.wait()


def expert_kernel(section, partners, offsets, capacity, group, split, unroll, info, *refs):
    @pl.when(info[0] == section)
    def _():
        expert_rows(partners, offsets, capacity, group, split, unroll, *refs)


def expert_rows(partners, offsets, capacity, group, split, unroll, *refs):
    halves, first = [], 0
    for pieces in split:
        halves.append(refs[first : first + pieces])
        first += pieces
    sent, outs = refs[first : first + partners], refs[-10 - partners : -10]
    numbers, places, placed, weights, arrived, state, hidden, total, made, left = refs[-10:]
    blocks = state.shape[0]
    padded = state.shape[1] // partners
    columns = (weights.shape[1] - 1) // 3
    count = group * capacity
    sizes = [columns] * 3 + [1]

    def part_of(k, number):
        return sent[k][number * count : (number + 1) * count, :]

    def load(half, which):
        source, start = halves[half][0], which * columns
        if len(halves[half]) > 1:
            source, start = halves[half][min(which, 2)], columns if which == 3 else 0
        return pltpu.make_async_copy(
            source.at[pl.ds(start, sizes[which])],
            weights.at[half, pl.ds(which * columns, sizes[which])],
            arrived.at[half, which],
        )

    for which in (3,), (0, 1), (2,):
        for half in range(len(halves)):
            for piece in which:
                load(half, piece).start()

    shape = (group * padded, count)
    block, slot = split_by(iota((group * padded, 1), 0), padded)
    key = jnp.where(slot < capacity, block * capacity + slot, -1)
    spread = jnp.where(iota(shape, 1) == key, 1.0, 0.0).astype(jnp.bfloat16)
    for number in range(blocks // group):
        spaced = side_by_side(
            spread, [p[at + number * count : at + (number + 1) * count, :] for p, at in zip(sent, offsets)]
        )
        for j in range(group):
            rows = jnp.concatenate([s[j * padded : (j + 1) * padded, :] for s in spaced], axis=0)
            state[number * group + j] = rows.astype(jnp.bfloat16)
            total[number * group + j] = jnp.zeros(rows.shape, jnp.float32)

    for half in range(len(halves)):
        load(half, 3).wait()
        numbers[half] = weights[half, 3 * columns, :16, :].astype(jnp.float32)[:8, :].astype(jnp.int32)
    moves = [pltpu.make_async_copy(numbers.at[half], places.at[half], placed.at[half]) for half in range(len(halves))]
    for move in moves:
        move.start()
    for move in moves:
        move.wait()

    for half in range(len(halves)):
        load(half, 0).wait()
        load(half, 1).wait()

        def up_step(at, carry, half=half):
            for i in range(unroll):
                c = at * unroll + i
                rows = state[places[half, 0, c]]
                both = dot(rows, jnp.concatenate([weights[half, c], weights[half, columns + c]], axis=1))
                gate, up = both[:, :LANES], both[:, LANES:]
                hidden[half * columns + c] = (gate / (1.0 + jnp.exp(-gate)) * up).astype(jnp.bfloat16)
            return carry

        lax.fori_loop(0, columns // unroll, up_step, 0)

    for half in range(len(halves)):
        load(half, 2).wait()

        def down_step(at, carry, half=half):
            produced = []
            for i in range(unroll):
                c = at * unroll + i
                produced.append(dot(hidden[half * columns + c], weights[half, 2 * columns + c]))
            for i in range(unroll):
                to = places[half, 1, at * unroll + i]
                total[to] = total[to] + produced[i]
            return carry

        lax.fori_loop(0, columns // unroll, down_step, 0)

    block, slot = split_by(iota((count, 1), 0), capacity)
    packing = jnp.where(iota((count, group * padded), 1) == block * padded + slot, 1.0, 0.0).astype(jnp.bfloat16)
    copies = [pltpu.make_async_copy(made.at[k], outs[k], left.at[k]) for k in range(partners)]
    for number in range(blocks // group):
        spaced = [
            jnp.concatenate(
                [total[number * group + j, k * padded : (k + 1) * padded, :] for j in range(group)], axis=0
            ).astype(jnp.bfloat16)
            for k in range(partners)
        ]
        for k, rows in enumerate(side_by_side(packing, spaced)):
            made[k, number * count : (number + 1) * count, :] = rows.astype(jnp.bfloat16)
    for copy in copies:
        copy.start()
    for copy in copies:
        copy.wait()


def pack_kernel(info, in_rows, out_cols, *refs):
    stored, (out, kept, numbers, named, arrived, left) = refs[:3], refs[-6:]
    columns = stored[0].shape[0]
    names = [
        pltpu.make_async_copy(source, numbers.at[at], named.at[at]) for at, source in enumerate((in_rows, out_cols))
    ]

    def take(at):
        return pltpu.make_async_copy(stored[at], kept.at[pl.ds(at * columns, columns)], arrived.at[at])

    def give(at):
        span = pl.ds(at * columns, columns + at // 2)
        return pltpu.make_async_copy(kept.at[span], out.at[span], left.at[at])

    for name in names:
        name.start()
    for at in range(3):
        take(at).start()
    spread = jnp.where(iota((columns, LANES), 0) == iota((columns, LANES), 1), 1.0, 0.0).astype(jnp.bfloat16)
    row = iota((LANES, LANES), 0)
    for name in names:
        name.wait()
    rows, cols = (
        dot(jnp.broadcast_to(numbers[at].astype(jnp.float32), (LANES, columns)).astype(jnp.bfloat16), spread)
        for at in range(2)
    )
    kept[3 * columns] = jnp.where(row == 0, rows, jnp.where(row == 1, cols, 0.0)).astype(jnp.bfloat16)
    for at in range(3):
        take(at).wait()
        give(at).start()
    for at in range(3):
        give(at).wait()


def tie_kernel(*refs):
    pass


SMEM = pl.BlockSpec(memory_space=pltpu.SMEM)
VMEM = pl.BlockSpec(memory_space=pltpu.VMEM)
ANY = pl.BlockSpec(memory_space=pl.ANY)


def held(*arrays):
    return [pltpu.with_memory_space_constraint(a, pltpu.HBM) for a in arrays]


def pack(info, places, weights, after):
    columns, *block = weights[0].shape
    shape = (3 * columns + 1, *block)
    return pl.pallas_call(
        pack_kernel,
        out_shape=pltpu.HBM(shape, jnp.bfloat16),
        in_specs=[SMEM] + [ANY] * (5 + len(after)),
        out_specs=ANY,
        scratch_shapes=[
            pltpu.VMEM(shape, jnp.bfloat16),
            pltpu.VMEM((2, 1, columns), jnp.int32),
            pltpu.SemaphoreType.DMA((2,)),
            pltpu.SemaphoreType.DMA((3,)),
            pltpu.SemaphoreType.DMA((3,)),
        ],
        compiler_params=pltpu.CompilerParams(vmem_limit_bytes=8 * MIB),
        name="pack",
    )(info, *held(*places, *weights), *after)


def tie(array, *others):
    return pl.pallas_call(
        tie_kernel,
        out_shape=pltpu.HBM(array.shape, array.dtype),
        in_specs=[ANY] * (1 + len(others)),
        out_specs=ANY,
        input_output_aliases={0: 0},
        name="tie",
    )(*held(array), *others)


def body(tokens, norm_gain, route_ids, route_weights, gate_blocks, up_blocks, down_blocks, gate_rows, down_cols):
    partners = lax.axis_size("expert")
    sections = lax.axis_size("section")
    shards = lax.axis_size("shard")
    micro_count, row_count, width = tokens.shape
    assert sections == 2 and gate_blocks.shape[1] == 1 and partners & (partners - 1) == 0
    assert lax.axis_size("groups") == 2
    blocks = width // LANES
    capacity = min(row_count, max(row_count * 9 // 16, row_count * TOP // partners + 2))
    group = group_of(capacity)
    size = blocks * capacity
    padded = up_to(capacity, 8)
    bf16, f32 = jnp.bfloat16, jnp.float32
    rows_shape = jax.ShapeDtypeStruct((size, LANES), bf16)
    carry_shape = pltpu.HBM((sections, size + blocks * row_count, LANES), bf16)
    state_shape = jax.ShapeDtypeStruct((row_count, width), bf16)
    info = jnp.stack([lax.axis_index(a) for a in ("section", "expert")]).astype(jnp.int32)
    weights = [a.reshape(a.shape[2:3] + a.shape[4:]) for a in (gate_blocks, up_blocks, down_blocks)]
    places = [a.reshape(1, -1) for a in (gate_rows, down_cols)]
    ids, shares = jnp.swapaxes(route_ids, 2, 3), jnp.swapaxes(route_weights, 2, 3)
    axes = ("groups", "shard", "expert", "section")
    sizes = [lax.axis_size(a) for a in axes]

    def trade(array, *moves):
        pairs = []
        for place in itertools.product(*(range(n) for n in sizes)):
            if moves[place[3]]:
                target = moves[place[3]](*place)
                pairs.append(tuple(sum(p * math.prod(sizes[i + 1 :]) for i, p in enumerate(q)) for q in (place, target)))
        return lax.ppermute(array, axes, pairs)

    def idle(g, s, e, c):
        return g ^ 1, s, e, c

    def to_partner(k):
        return lambda g, s, e, c: (g, s, e ^ k, c)

    def to_next(k):
        return lambda g, s, e, c: (g, s, e ^ k, 1)

    def idle_back(g, s, e, c):
        return g ^ 1, s, e, 0

    def across(g, s, e, c):
        return g, s ^ 1, e, c

    def exchange(parts, *moves_of):
        moved = list(parts)
        for k in range(partners - 1, 0, -1):
            moved[k] = trade(parts[k], *(m(k) for m in moves_of))
        return moved

    def swap(array):
        return lax.ppermute(array, "section", [(0, 1), (1, 0)])

    def always(move):
        return lambda k: move

    paired = shards == 2
    if not paired:
        weights = [lax.all_gather(a, "shard", axis=0, tiled=True) for a in weights]
        places = [lax.all_gather(a, "shard", axis=1, tiled=True) for a in places]
    columns = weights[0].shape[0]
    assert columns <= LANES

    def call(kernel, name, out_shape, args, specs, scratch, limit, out_specs=None, aliases={}):
        return pl.pallas_call(
            kernel,
            out_shape=out_shape,
            in_specs=specs,
            out_specs=out_specs or [VMEM] * len(out_shape),
            scratch_shapes=scratch,
            input_output_aliases=aliases,
            compiler_params=pltpu.CompilerParams(vmem_limit_bytes=limit * MIB),
            name=name,
        )(*args)

    def expert(layer, sources, rows, offsets, after):
        return call(
            functools.partial(
                expert_kernel, layer, partners, offsets, capacity, group, [1] * len(sources), math.gcd(columns, 32)
            ),
            "expert",
            [pltpu.HBM(rows_shape.shape, bf16)] * partners,
            (info, *held(*sources), *rows, *after),
            [SMEM] + [ANY] * len(sources) + [VMEM] * partners + [ANY] * len(after),
            [
                pltpu.VMEM((len(sources), 8, LANES), jnp.int32),
                pltpu.SMEM((len(sources), 8, LANES), jnp.int32),
                pltpu.SemaphoreType.DMA((len(sources),)),
                pltpu.VMEM((len(sources), 3 * columns + 1) + weights[0].shape[1:], bf16),
                pltpu.SemaphoreType.DMA((len(sources), 4)),
                pltpu.VMEM((blocks, partners * padded, LANES), bf16),
                pltpu.VMEM((len(sources) * columns, partners * padded, LANES), bf16),
                pltpu.VMEM((blocks, partners * padded, LANES), f32),
                pltpu.VMEM((partners,) + rows_shape.shape, bf16),
                pltpu.SemaphoreType.DMA((partners,)),
            ],
            22,
            [ANY] * partners,
        )

    packed = pack(info, places, weights, [])
    next_ids, next_gain = swap(ids), swap(norm_gain)
    sent = call(
        functools.partial(first_send_kernel, partners, capacity, group),
        "first_send",
        [jax.ShapeDtypeStruct((micro_count * size, LANES), bf16)] * partners,
        (info, *held(tokens), ids, norm_gain, next_ids, next_gain),
        [SMEM, ANY, VMEM, VMEM, ANY, ANY],
        [
            pltpu.VMEM(tokens.shape, bf16),
            pltpu.VMEM((blocks * row_count, LANES), bf16),
            pltpu.SemaphoreType.DMA((1,)),
        ],
        16,
    )
    rows = exchange(sent, to_partner, always(None))
    sources = [[packed], [packed]]
    if paired:
        moved = tie(trade(packed, across, idle), *rows[1:])
        packed = tie(packed, moved)
        arrived = trade(packed, None, across)
        sources = [[packed, moved], [packed, arrived]]
    after = []
    back = []
    for micro in range(micro_count):
        done = expert(0, sources[0], rows, [micro * size] * partners, after)
        after = held(done[0])
        back.append(exchange(done, to_partner, always(idle)))
    firsts, carries, given_rows = [], [], []
    for micro in range(micro_count):
        first, carry, *sent = call(
            functools.partial(relay_kernel, micro, partners, capacity, group),
            "relay",
            [pltpu.HBM(state_shape.shape, bf16), carry_shape] + [rows_shape] * (partners - 1),
            (info, *held(tokens), ids, shares, next_ids, next_gain, *held(back[micro][0]), *back[micro][1:], *after),
            [SMEM, ANY] + [VMEM] * (4 + partners) + [ANY] * len(after),
            [pltpu.VMEM((row_count, width), bf16), pltpu.SemaphoreType.DMA((1,))],
            12,
        )
        after = held(first)
        firsts.append(first)
        carries.append(carry)
        given_rows.append(exchange([carry] + sent, to_next, always(idle_back)))
    carries = [
        lax.all_to_all(carry, "section", split_axis=0, concat_axis=0, tiled=True).reshape(-1, LANES) for carry in carries
    ]
    given_rows = [[carry] + parts[1:] for carry, parts in zip(carries, given_rows)]
    after = held(first)
    back = []
    for micro in range(micro_count):
        done = expert(1, sources[1], given_rows[micro], [0] * partners, after)
        after = [swap(done[0])]
        back.append(exchange(done, always(idle), to_partner))
    out = None
    for micro in range(micro_count):
        kept = [] if out is None else held(out)
        out = call(
            functools.partial(last_kernel, micro, partners, capacity, group),
            "last",
            pltpu.HBM((1, micro_count, row_count, width), bf16),
            (
                info,
                *held(firsts[micro]),
                carries[micro],
                ids,
                shares,
                *held(back[micro][0]),
                *back[micro][1:],
                *kept,
            ),
            [SMEM, ANY] + [VMEM] * (3 + partners) + [ANY] * len(kept),
            [pltpu.VMEM((row_count, width), bf16), pltpu.SemaphoreType.DMA((2,))],
            12,
            ANY,
            {5 + partners: 0} if kept else {},
        )
    return out


def solution(mesh):
    in_specs = (
        P(None, ("groups", "shard", "expert"), None),
        P("section", None),
        P("section", None, ("groups", "shard", "expert"), None),
        P("section", None, ("groups", "shard", "expert"), None),
        P("section", "expert", "shard", None, None, None),
        P("section", "expert", "shard", None, None, None),
        P("section", "expert", "shard", None, None, None),
        P("section", "expert", "shard", None),
        P("section", "expert", "shard", None),
    )
    out_specs = P("section", None, ("groups", "shard", "expert"), None)
    return jax.shard_map(body, mesh=mesh, in_specs=in_specs, out_specs=out_specs, check_vma=False)
```

```python
import functools
import itertools
import math

import jax
import jax.numpy as jnp
from jax import lax
from jax.experimental import pallas as pl
from jax.experimental.pallas import tpu as pltpu
from jax.sharding import PartitionSpec as P

TOP = 2
LANES = 128
EPS = 1e-05
MIB = 1 << 20


def up_to(value, unit):
    return -(-value // unit) * unit


def group_of(capacity):
    return 16 // math.gcd(capacity, 16)


def iota(shape, axis):
    return lax.broadcasted_iota(jnp.int32, shape, axis)


def split_by(values, unit):
    quotient = jnp.floor((values.astype(jnp.float32) + 0.5) * (1.0 / unit)).astype(jnp.int32)
    return quotient, values - quotient * unit


def dot(left, right, contract=((1,), (0,))):
    return lax.dot_general(left, right, (contract, ((), ())), preferred_element_type=jnp.float32)


def side_by_side(left, rights):
    products = []
    for at in range(0, len(rights), 2):
        pair = rights[at : at + 2]
        product = dot(left, jnp.concatenate(pair, axis=1))
        products += [product[:, i * LANES : (i + 1) * LANES] for i in range(len(pair))]
    return products


def spread_columns(values, rows):
    tokens = values.shape[1]
    token = split_by(iota((rows, tokens), 0), tokens)[1]
    same = iota((rows, tokens), 1) == token
    return [
        jnp.sum(jnp.where(same, values[choice : choice + 1, :], 0.0), axis=1, keepdims=True) for choice in range(TOP)
    ]


def picks_to_send(ids, experts, capacity, group):
    tokens = ids.shape[1]
    expert = iota((up_to(experts, 16), tokens), 0)
    hit = (ids[0:1, :] == expert) | (ids[1:2, :] == expert)
    hit = jnp.where(hit, 1.0, 0.0).astype(jnp.bfloat16)
    shape = (tokens, group * tokens)
    block, token = split_by(iota(shape, 1), tokens)
    earlier = jnp.where(iota(shape, 0) < token, 1.0, 0.0).astype(jnp.bfloat16)
    same = jnp.where(iota(shape, 0) == token, 1.0, 0.0).astype(jnp.bfloat16)
    slot = dot(hit, earlier)
    here = dot(hit, same)
    first = (block[0:1, :] * capacity).astype(jnp.float32)
    key = jnp.where(here > 0.5, slot + first, -1.0)
    row = iota((group * capacity, group * tokens), 0).astype(jnp.float32)
    return jnp.concatenate(
        [jnp.where(row == key[k : k + 1, :], 1.0, 0.0) for k in range(experts)], axis=0
    ).astype(jnp.bfloat16)


def picks_to_mix(ids, experts, capacity, group):
    tokens = ids.shape[1]
    rows = group * tokens
    token = split_by(iota((rows, tokens), 0), tokens)[1]
    first = (split_by(iota((rows, 1), 0), tokens)[0] * capacity).astype(jnp.float32)
    columns = iota((rows, experts * group * capacity), 1).astype(jnp.float32)
    earlier = iota((rows, tokens), 1) < token
    chosen = spread_columns(ids.astype(jnp.float32), rows)
    parts = []
    for choice in range(TOP):
        expert = chosen[choice]
        named = (ids[0:1, :].astype(jnp.float32) == expert) | (ids[1:2, :].astype(jnp.float32) == expert)
        slot = jnp.sum(jnp.where(named & earlier, 1.0, 0.0), axis=1, keepdims=True)
        key = expert * (group * capacity) + first + slot
        parts.append(jnp.where(columns == key, 1.0, 0.0))
    return jnp.concatenate(parts, axis=0).astype(jnp.bfloat16)


def send_rows(partners, state, scale, gain_of, outs, group, capacity, tokens):
    count = group * capacity
    blocks = state.shape[0] // tokens
    picks = picks_to_send(partners, len(outs), capacity, group)
    scale = jnp.concatenate([scale] * group, axis=0)
    normed = []
    for number in range(blocks // group):
        rows = state[number * group * tokens : (number + 1) * group * tokens, :]
        gain = jnp.concatenate(
            [jnp.broadcast_to(gain_of(number * group + j), (tokens, LANES)) for j in range(group)], axis=0
        )
        normed.append((rows.astype(jnp.float32) * scale * gain).astype(jnp.bfloat16))
    for number, picked in enumerate(side_by_side(picks, normed)):
        for k, out in enumerate(outs):
            out[number * count : (number + 1) * count, :] = picked[k * count : (k + 1) * count, :].astype(jnp.bfloat16)


def first_send_kernel(partners, capacity, group, info, tokens_ref, ids, gain, *rest):
    outs, (given, state, arrived) = rest[-partners - 3 : -3], rest[-3:]

    @pl.when(info[0] == 0)
    def _():
        copy = pltpu.make_async_copy(tokens_ref, given, arrived.at[0])
        copy.start()
        copy.wait()
        micro_count, tokens, width = given.shape
        blocks = width // LANES
        for micro in range(micro_count):
            total = jnp.zeros((tokens, 1), jnp.float32)
            for b in range(blocks):
                part = given[micro, :, b * LANES : (b + 1) * LANES]
                state[b * tokens : (b + 1) * tokens, :] = part
                wide = part.astype(jnp.float32)
                total += jnp.sum(wide * wide, axis=1, keepdims=True)
            scale = lax.rsqrt(total * (1.0 / width) + EPS)
            size = blocks * capacity
            targets = [out.at[micro * size : (micro + 1) * size, :] for out in outs]
            send_rows(ids[0, micro] ^ info[1], state, scale, lambda b: gain_of(gain, b), targets, group, capacity, tokens)


def gain_of(gain, block):
    return gain[0:1, block * LANES : (block + 1) * LANES]


def mix_rows(picks, base_of, weights, returned, blocks, group, capacity, tokens):
    count, rows = group * capacity, group * tokens
    given = [
        jnp.concatenate([part[number * count : (number + 1) * count, :] for part in returned], axis=0)
        for number in range(blocks // group)
    ]
    for number, picked in enumerate(side_by_side(picks, given)):
        total = base_of(number).astype(jnp.float32)
        for choice in range(TOP):
            total += weights[choice] * picked[choice * rows : (choice + 1) * rows, :]
        yield number, total.astype(jnp.bfloat16)


def relay_kernel(micro, partners, capacity, group, info, *refs):
    @pl.when(info[0] == 0)
    def _():
        relay_rows(micro, partners, capacity, group, info, *refs)


def relay_rows(micro, partners, capacity, group, info, tokens_ref, ids, weights, next_ids, next_gain, *rest):
    returned, (state_to, carry_to), outs = rest[:partners], rest[-partners - 7 : -partners - 5], rest[-partners - 5 : -6]
    given, arrived, state_out, carried, made, left = rest[-6:]
    copy = pltpu.make_async_copy(tokens_ref.at[micro], given, arrived.at[0])
    copy.start()
    tokens, width = given.shape
    blocks = width // LANES
    state = carried.at[blocks * capacity : blocks * (capacity + tokens), :]
    picks = picks_to_mix(ids[0, micro] ^ info[1], partners, capacity, group)
    shares = spread_columns(weights[0, micro], group * tokens)
    total = jnp.zeros((tokens, 1), jnp.float32)
    copy.wait()

    def base_of(number):
        return jnp.concatenate(
            [given[:, b * LANES : (b + 1) * LANES] for b in range(number * group, (number + 1) * group)], axis=0
        )

    for number, mixed in mix_rows(picks, base_of, shares, returned, blocks, group, capacity, tokens):
        state[number * group * tokens : (number + 1) * group * tokens, :] = mixed
        wide = mixed.astype(jnp.float32)
        square = jnp.sum(wide * wide, axis=1, keepdims=True)
        for j in range(group):
            b = number * group + j
            state_out[:, b * LANES : (b + 1) * LANES] = mixed[j * tokens : (j + 1) * tokens, :]
            total += square[j * tokens : (j + 1) * tokens, :]
    scale = lax.rsqrt(total * (1.0 / width) + EPS)
    own = blocks * capacity
    copies = [pltpu.make_async_copy(state_out, state_to, left.at[0])]
    copies += [pltpu.make_async_copy(carried.at[pl.ds(own, state.shape[0])], carry_to.at[1, pl.ds(own, state.shape[0])], left.at[1])]
    for copy in copies:
        copy.start()
    targets = [carried] + [made.at[k] for k in range(partners - 1)]
    send_rows(
        next_ids[0, micro] ^ info[1], state, scale, lambda b: gain_of(next_gain, b), targets, group, capacity, tokens
    )
    sends = [pltpu.make_async_copy(made.at[k], outs[k], left.at[3 + k]) for k in range(partners - 1)]
    sends += [pltpu.make_async_copy(carried.at[pl.ds(0, own)], carry_to.at[1, pl.ds(0, own)], left.at[2])]
    for copy in sends:
        copy.start()
    for copy in copies + sends:
        copy.wait()


def last_kernel(micro, partners, capacity, group, info, first, carried, ids, weights, *rest):
    returned, (out, made, done) = rest[:partners], rest[-3:]
    tokens, width = made.shape
    blocks = width // LANES
    keep = pltpu.make_async_copy(made, out.at[0, micro], done.at[0])

    @pl.when(info[0] == 0)
    def _():
        copy = pltpu.make_async_copy(first, made, done.at[1])
        copy.start()
        copy.wait()

    @pl.when(info[0] != 0)
    def _():
        picks = picks_to_mix(ids[0, micro] ^ info[1], partners, capacity, group)
        shares = spread_columns(weights[0, micro], group * tokens)

        def base_of(number):
            start = blocks * capacity + number * group * tokens
            return carried[start : start + group * tokens, :]

        for number, mixed in mix_rows(picks, base_of, shares, returned, blocks, group, capacity, tokens):
            for j in range(group):
                b = number * group + j
                made[:, b * LANES : (b + 1) * LANES] = mixed[j * tokens : (j + 1) * tokens, :]

    keep.start()
    keep.wait()


def expert_kernel(section, partners, offsets, capacity, group, split, unroll, info, *refs):
    @pl.when(info[0] == section)
    def _():
        expert_rows(partners, offsets, capacity, group, split, unroll, *refs)


def expert_rows(partners, offsets, capacity, group, split, unroll, *refs):
    halves, first = [], 0
    for pieces in split:
        halves.append(refs[first : first + pieces])
        first += pieces
    sent, outs = refs[first : first + partners], refs[-10 - partners : -10]
    numbers, places, placed, weights, arrived, state, hidden, total, made, left = refs[-10:]
    blocks = state.shape[0]
    padded = state.shape[1] // partners
    columns = (weights.shape[1] - 1) // 3
    count = group * capacity
    sizes = [columns] * 3 + [1]

    def part_of(k, number):
        return sent[k][number * count : (number + 1) * count, :]

    def load(half, which):
        source, start = halves[half][0], which * columns
        if len(halves[half]) > 1:
            source, start = halves[half][min(which, 2)], columns if which == 3 else 0
        return pltpu.make_async_copy(
            source.at[pl.ds(start, sizes[which])],
            weights.at[half, pl.ds(which * columns, sizes[which])],
            arrived.at[half, which],
        )

    for which in (3,), (0, 1), (2,):
        for half in range(len(halves)):
            for piece in which:
                load(half, piece).start()

    shape = (group * padded, count)
    block, slot = split_by(iota((group * padded, 1), 0), padded)
    key = jnp.where(slot < capacity, block * capacity + slot, -1)
    spread = jnp.where(iota(shape, 1) == key, 1.0, 0.0).astype(jnp.bfloat16)
    for number in range(blocks // group):
        spaced = side_by_side(
            spread, [p[at + number * count : at + (number + 1) * count, :] for p, at in zip(sent, offsets)]
        )
        for j in range(group):
            rows = jnp.concatenate([s[j * padded : (j + 1) * padded, :] for s in spaced], axis=0)
            state[number * group + j] = rows.astype(jnp.bfloat16)
            total[number * group + j] = jnp.zeros(rows.shape, jnp.float32)

    for half in range(len(halves)):
        load(half, 3).wait()
        numbers[half] = weights[half, 3 * columns, :16, :].astype(jnp.float32)[:8, :].astype(jnp.int32)
    moves = [pltpu.make_async_copy(numbers.at[half], places.at[half], placed.at[half]) for half in range(len(halves))]
    for move in moves:
        move.start()
    for move in moves:
        move.wait()

    for half in range(len(halves)):
        load(half, 0).wait()
        load(half, 1).wait()

        def up_step(at, carry, half=half):
            for i in range(unroll):
                c = at * unroll + i
                rows = state[places[half, 0, c]]
                both = dot(rows, jnp.concatenate([weights[half, c], weights[half, columns + c]], axis=1))
                gate, up = both[:, :LANES], both[:, LANES:]
                hidden[half * columns + c] = (gate / (1.0 + jnp.exp(-gate)) * up).astype(jnp.bfloat16)
            return carry

        lax.fori_loop(0, columns // unroll, up_step, 0)

    for half in range(len(halves)):
        load(half, 2).wait()

        def down_step(at, carry, half=half):
            produced = []
            for i in range(unroll):
                c = at * unroll + i
                produced.append(dot(hidden[half * columns + c], weights[half, 2 * columns + c]))
            for i in range(unroll):
                to = places[half, 1, at * unroll + i]
                total[to] = total[to] + produced[i]
            return carry

        lax.fori_loop(0, columns // unroll, down_step, 0)

    block, slot = split_by(iota((count, 1), 0), capacity)
    packing = jnp.where(iota((count, group * padded), 1) == block * padded + slot, 1.0, 0.0).astype(jnp.bfloat16)
    copies = [pltpu.make_async_copy(made.at[k], outs[k], left.at[k]) for k in range(partners)]
    for number in range(blocks // group):
        spaced = [
            jnp.concatenate(
                [total[number * group + j, k * padded : (k + 1) * padded, :] for j in range(group)], axis=0
            ).astype(jnp.bfloat16)
            for k in range(partners)
        ]
        for k, rows in enumerate(side_by_side(packing, spaced)):
            made[k, number * count : (number + 1) * count, :] = rows.astype(jnp.bfloat16)
    for copy in copies:
        copy.start()
    for copy in copies:
        copy.wait()


def pack_kernel(info, in_rows, out_cols, *refs):
    stored, (out, kept, numbers, named, arrived, left) = refs[:3], refs[-6:]
    columns = stored[0].shape[0]
    names = [
        pltpu.make_async_copy(source, numbers.at[at], named.at[at]) for at, source in enumerate((in_rows, out_cols))
    ]

    def take(at):
        return pltpu.make_async_copy(stored[at], kept.at[pl.ds(at * columns, columns)], arrived.at[at])

    def give(at):
        span = pl.ds(at * columns, columns + at // 2)
        return pltpu.make_async_copy(kept.at[span], out.at[span], left.at[at])

    for name in names:
        name.start()
    for at in range(3):
        take(at).start()
    spread = jnp.where(iota((columns, LANES), 0) == iota((columns, LANES), 1), 1.0, 0.0).astype(jnp.bfloat16)
    row = iota((LANES, LANES), 0)
    for name in names:
        name.wait()
    rows, cols = (
        dot(jnp.broadcast_to(numbers[at].astype(jnp.float32), (LANES, columns)).astype(jnp.bfloat16), spread)
        for at in range(2)
    )
    kept[3 * columns] = jnp.where(row == 0, rows, jnp.where(row == 1, cols, 0.0)).astype(jnp.bfloat16)
    for at in range(3):
        take(at).wait()
        give(at).start()
    for at in range(3):
        give(at).wait()


def tie_kernel(*refs):
    pass


SMEM = pl.BlockSpec(memory_space=pltpu.SMEM)
VMEM = pl.BlockSpec(memory_space=pltpu.VMEM)
ANY = pl.BlockSpec(memory_space=pl.ANY)


def held(*arrays):
    return [pltpu.with_memory_space_constraint(a, pltpu.HBM) for a in arrays]


def pack(info, places, weights, after):
    columns, *block = weights[0].shape
    shape = (3 * columns + 1, *block)
    return pl.pallas_call(
        pack_kernel,
        out_shape=pltpu.HBM(shape, jnp.bfloat16),
        in_specs=[SMEM] + [ANY] * (5 + len(after)),
        out_specs=ANY,
        scratch_shapes=[
            pltpu.VMEM(shape, jnp.bfloat16),
            pltpu.VMEM((2, 1, columns), jnp.int32),
            pltpu.SemaphoreType.DMA((2,)),
            pltpu.SemaphoreType.DMA((3,)),
            pltpu.SemaphoreType.DMA((3,)),
        ],
        compiler_params=pltpu.CompilerParams(vmem_limit_bytes=8 * MIB),
        name="pack",
    )(info, *held(*places, *weights), *after)


def tie(array, *others):
    return pl.pallas_call(
        tie_kernel,
        out_shape=pltpu.HBM(array.shape, array.dtype),
        in_specs=[ANY] * (1 + len(others)),
        out_specs=ANY,
        input_output_aliases={0: 0},
        name="tie",
    )(*held(array), *others)


def body(tokens, norm_gain, route_ids, route_weights, gate_blocks, up_blocks, down_blocks, gate_rows, down_cols):
    partners = lax.axis_size("expert")
    sections = lax.axis_size("section")
    shards = lax.axis_size("shard")
    micro_count, row_count, width = tokens.shape
    assert sections == 2 and gate_blocks.shape[1] == 1 and partners & (partners - 1) == 0
    assert lax.axis_size("groups") == 2
    blocks = width // LANES
    capacity = min(row_count, max(row_count * 9 // 16, row_count * TOP // partners + 2))
    group = group_of(capacity)
    size = blocks * capacity
    padded = up_to(capacity, 8)
    bf16, f32 = jnp.bfloat16, jnp.float32
    rows_shape = jax.ShapeDtypeStruct((size, LANES), bf16)
    carry_shape = pltpu.HBM((sections, size + blocks * row_count, LANES), bf16)
    state_shape = jax.ShapeDtypeStruct((row_count, width), bf16)
    info = jnp.stack([lax.axis_index(a) for a in ("section", "expert")]).astype(jnp.int32)
    weights = [a.reshape(a.shape[2:3] + a.shape[4:]) for a in (gate_blocks, up_blocks, down_blocks)]
    places = [a.reshape(1, -1) for a in (gate_rows, down_cols)]
    ids, shares = jnp.swapaxes(route_ids, 2, 3), jnp.swapaxes(route_weights, 2, 3)
    axes = ("groups", "shard", "expert", "section")
    sizes = [lax.axis_size(a) for a in axes]

    def trade(array, *moves):
        pairs = []
        for place in itertools.product(*(range(n) for n in sizes)):
            if moves[place[3]]:
                target = moves[place[3]](*place)
                pairs.append(tuple(sum(p * math.prod(sizes[i + 1 :]) for i, p in enumerate(q)) for q in (place, target)))
        return lax.ppermute(array, axes, pairs)

    def idle(g, s, e, c):
        return g ^ 1, s, e, c

    def to_partner(k):
        return lambda g, s, e, c: (g, s, e ^ k, c)

    def to_next(k):
        return lambda g, s, e, c: (g, s, e ^ k, 1)

    def idle_back(g, s, e, c):
        return g ^ 1, s, e, 0

    def across(g, s, e, c):
        return g, s ^ 1, e, c

    def exchange(parts, *moves_of):
        moved = list(parts)
        for k in range(partners - 1, 0, -1):
            moved[k] = trade(parts[k], *(m(k) for m in moves_of))
        return moved

    def swap(array):
        return lax.ppermute(array, "section", [(0, 1), (1, 0)])

    def always(move):
        return lambda k: move

    paired = shards == 2
    if not paired:
        weights = [lax.all_gather(a, "shard", axis=0, tiled=True) for a in weights]
        places = [lax.all_gather(a, "shard", axis=1, tiled=True) for a in places]
    columns = weights[0].shape[0]
    assert columns <= LANES

    def call(kernel, name, out_shape, args, specs, scratch, limit, out_specs=None, aliases={}):
        return pl.pallas_call(
            kernel,
            out_shape=out_shape,
            in_specs=specs,
            out_specs=out_specs or [VMEM] * len(out_shape),
            scratch_shapes=scratch,
            input_output_aliases=aliases,
            compiler_params=pltpu.CompilerParams(vmem_limit_bytes=limit * MIB),
            name=name,
        )(*args)

    def expert(layer, sources, rows, offsets, after):
        return call(
            functools.partial(
                expert_kernel, layer, partners, offsets, capacity, group, [1] * len(sources), math.gcd(columns, 32)
            ),
            "expert",
            [pltpu.HBM(rows_shape.shape, bf16)] * partners,
            (info, *held(*sources), *rows, *after),
            [SMEM] + [ANY] * len(sources) + [VMEM] * partners + [ANY] * len(after),
            [
                pltpu.VMEM((len(sources), 8, LANES), jnp.int32),
                pltpu.SMEM((len(sources), 8, LANES), jnp.int32),
                pltpu.SemaphoreType.DMA((len(sources),)),
                pltpu.VMEM((len(sources), 3 * columns + 1) + weights[0].shape[1:], bf16),
                pltpu.SemaphoreType.DMA((len(sources), 4)),
                pltpu.VMEM((blocks, partners * padded, LANES), bf16),
                pltpu.VMEM((len(sources) * columns, partners * padded, LANES), bf16),
                pltpu.VMEM((blocks, partners * padded, LANES), f32),
                pltpu.VMEM((partners,) + rows_shape.shape, bf16),
                pltpu.SemaphoreType.DMA((partners,)),
            ],
            22,
            [ANY] * partners,
        )

    packed = pack(info, places, weights, [])
    next_ids, next_gain = swap(ids), swap(norm_gain)
    sent = call(
        functools.partial(first_send_kernel, partners, capacity, group),
        "first_send",
        [jax.ShapeDtypeStruct((micro_count * size, LANES), bf16)] * partners,
        (info, *held(tokens), ids, norm_gain, next_ids, next_gain),
        [SMEM, ANY, VMEM, VMEM, ANY, ANY],
        [
            pltpu.VMEM(tokens.shape, bf16),
            pltpu.VMEM((blocks * row_count, LANES), bf16),
            pltpu.SemaphoreType.DMA((1,)),
        ],
        16,
    )
    rows = exchange(sent, to_partner, always(None))
    sources = [[packed], [packed]]
    if paired:
        moved = tie(trade(packed, across, idle), *rows[1:])
        packed = tie(packed, moved)
        arrived = trade(packed, None, across)
        sources = [[packed, moved], [packed, arrived]]
    after = []
    back = []
    for micro in range(micro_count):
        done = expert(0, sources[0], rows, [micro * size] * partners, after)
        after = held(done[0])
        back.append(exchange(done, to_partner, always(idle)))
    firsts, carries, given_rows = [], [], []
    for micro in range(micro_count):
        first, carry, *sent = call(
            functools.partial(relay_kernel, micro, partners, capacity, group),
            "relay",
            [pltpu.HBM(state_shape.shape, bf16), carry_shape] + [pltpu.HBM(rows_shape.shape, bf16)] * (partners - 1),
            (info, *held(tokens), ids, shares, next_ids, next_gain, *held(back[micro][0]), *back[micro][1:], *after),
            [SMEM, ANY] + [VMEM] * (4 + partners) + [ANY] * len(after),
            [
                pltpu.VMEM((row_count, width), bf16),
                pltpu.SemaphoreType.DMA((1,)),
                pltpu.VMEM((row_count, width), bf16),
                pltpu.VMEM(carry_shape.shape[1:], bf16),
                pltpu.VMEM((partners - 1,) + rows_shape.shape, bf16),
                pltpu.SemaphoreType.DMA((partners + 2,)),
            ],
            12,
            [ANY] * (partners + 1),
        )
        after = held(first)
        firsts.append(first)
        carries.append(carry)
        given_rows.append(exchange([carry] + sent, to_next, always(idle_back)))
    carries = [
        lax.all_to_all(carry, "section", split_axis=0, concat_axis=0, tiled=True).reshape(-1, LANES) for carry in carries
    ]
    given_rows = [[carry] + parts[1:] for carry, parts in zip(carries, given_rows)]
    after = held(first)
    back = []
    for micro in range(micro_count):
        done = expert(1, sources[1], given_rows[micro], [0] * partners, after)
        after = [swap(done[0])]
        back.append(exchange(done, always(idle), to_partner))
    out = None
    for micro in range(micro_count):
        kept = [] if out is None else held(out)
        out = call(
            functools.partial(last_kernel, micro, partners, capacity, group),
            "last",
            pltpu.HBM((1, micro_count, row_count, width), bf16),
            (
                info,
                *held(firsts[micro]),
                carries[micro],
                ids,
                shares,
                *held(back[micro][0]),
                *back[micro][1:],
                *kept,
            ),
            [SMEM, ANY] + [VMEM] * (3 + partners) + [ANY] * len(kept),
            [pltpu.VMEM((row_count, width), bf16), pltpu.SemaphoreType.DMA((2,))],
            12,
            ANY,
            {5 + partners: 0} if kept else {},
        )
    return out


def solution(mesh):
    in_specs = (
        P(None, ("groups", "shard", "expert"), None),
        P("section", None),
        P("section", None, ("groups", "shard", "expert"), None),
        P("section", None, ("groups", "shard", "expert"), None),
        P("section", "expert", "shard", None, None, None),
        P("section", "expert", "shard", None, None, None),
        P("section", "expert", "shard", None, None, None),
        P("section", "expert", "shard", None),
        P("section", "expert", "shard", None),
    )
    out_specs = P("section", None, ("groups", "shard", "expert"), None)
    return jax.shard_map(body, mesh=mesh, in_specs=in_specs, out_specs=out_specs, check_vma=False)
```

```python
import functools
import itertools
import math

import jax
import jax.numpy as jnp
from jax import lax
from jax.experimental import pallas as pl
from jax.experimental.pallas import tpu as pltpu
from jax.sharding import PartitionSpec as P

TOP = 2
LANES = 128
EPS = 1e-05
MIB = 1 << 20


def up_to(value, unit):
    return -(-value // unit) * unit


def group_of(capacity):
    return 16 // math.gcd(capacity, 16)


def iota(shape, axis):
    return lax.broadcasted_iota(jnp.int32, shape, axis)


def split_by(values, unit):
    quotient = jnp.floor((values.astype(jnp.float32) + 0.5) * (1.0 / unit)).astype(jnp.int32)
    return quotient, values - quotient * unit


def dot(left, right, contract=((1,), (0,))):
    return lax.dot_general(left, right, (contract, ((), ())), preferred_element_type=jnp.float32)


def side_by_side(left, rights):
    products = []
    for at in range(0, len(rights), 2):
        pair = rights[at : at + 2]
        product = dot(left, jnp.concatenate(pair, axis=1))
        products += [product[:, i * LANES : (i + 1) * LANES] for i in range(len(pair))]
    return products


def spread_columns(values, rows):
    tokens = values.shape[1]
    token = split_by(iota((rows, tokens), 0), tokens)[1]
    same = iota((rows, tokens), 1) == token
    return [
        jnp.sum(jnp.where(same, values[choice : choice + 1, :], 0.0), axis=1, keepdims=True) for choice in range(TOP)
    ]


def picks_to_send(ids, experts, capacity, group):
    tokens = ids.shape[1]
    expert = iota((up_to(experts, 16), tokens), 0)
    hit = (ids[0:1, :] == expert) | (ids[1:2, :] == expert)
    hit = jnp.where(hit, 1.0, 0.0).astype(jnp.bfloat16)
    shape = (tokens, group * tokens)
    block, token = split_by(iota(shape, 1), tokens)
    earlier = jnp.where(iota(shape, 0) < token, 1.0, 0.0).astype(jnp.bfloat16)
    same = jnp.where(iota(shape, 0) == token, 1.0, 0.0).astype(jnp.bfloat16)
    slot = dot(hit, earlier)
    here = dot(hit, same)
    first = (block[0:1, :] * capacity).astype(jnp.float32)
    key = jnp.where(here > 0.5, slot + first, -1.0)
    row = iota((group * capacity, group * tokens), 0).astype(jnp.float32)
    return jnp.concatenate(
        [jnp.where(row == key[k : k + 1, :], 1.0, 0.0) for k in range(experts)], axis=0
    ).astype(jnp.bfloat16)


def picks_to_mix(ids, experts, capacity, group):
    tokens = ids.shape[1]
    rows = group * tokens
    token = split_by(iota((rows, tokens), 0), tokens)[1]
    first = (split_by(iota((rows, 1), 0), tokens)[0] * capacity).astype(jnp.float32)
    columns = iota((rows, experts * group * capacity), 1).astype(jnp.float32)
    earlier = iota((rows, tokens), 1) < token
    chosen = spread_columns(ids.astype(jnp.float32), rows)
    parts = []
    for choice in range(TOP):
        expert = chosen[choice]
        named = (ids[0:1, :].astype(jnp.float32) == expert) | (ids[1:2, :].astype(jnp.float32) == expert)
        slot = jnp.sum(jnp.where(named & earlier, 1.0, 0.0), axis=1, keepdims=True)
        key = expert * (group * capacity) + first + slot
        parts.append(jnp.where(columns == key, 1.0, 0.0))
    return jnp.concatenate(parts, axis=0).astype(jnp.bfloat16)


def send_rows(partners, state, scale, gain_of, outs, group, capacity, tokens):
    count = group * capacity
    blocks = state.shape[0] // tokens
    picks = picks_to_send(partners, len(outs), capacity, group)
    scale = jnp.concatenate([scale] * group, axis=0)
    normed = []
    for number in range(blocks // group):
        rows = state[number * group * tokens : (number + 1) * group * tokens, :]
        gain = jnp.concatenate(
            [jnp.broadcast_to(gain_of(number * group + j), (tokens, LANES)) for j in range(group)], axis=0
        )
        normed.append((rows.astype(jnp.float32) * scale * gain).astype(jnp.bfloat16))
    for number, picked in enumerate(side_by_side(picks, normed)):
        for k, out in enumerate(outs):
            out[number * count : (number + 1) * count, :] = picked[k * count : (k + 1) * count, :].astype(jnp.bfloat16)


def first_send_kernel(partners, capacity, group, info, tokens_ref, ids, gain, *rest):
    outs, (given, state, arrived) = rest[-partners - 3 : -3], rest[-3:]

    @pl.when(info[0] == 0)
    def _():
        copy = pltpu.make_async_copy(tokens_ref, given, arrived.at[0])
        copy.start()
        copy.wait()
        micro_count, tokens, width = given.shape
        blocks = width // LANES
        for micro in range(micro_count):
            total = jnp.zeros((tokens, 1), jnp.float32)
            for b in range(blocks):
                part = given[micro, :, b * LANES : (b + 1) * LANES]
                state[b * tokens : (b + 1) * tokens, :] = part
                wide = part.astype(jnp.float32)
                total += jnp.sum(wide * wide, axis=1, keepdims=True)
            scale = lax.rsqrt(total * (1.0 / width) + EPS)
            size = blocks * capacity
            targets = [out.at[micro * size : (micro + 1) * size, :] for out in outs]
            send_rows(ids[0, micro] ^ info[1], state, scale, lambda b: gain_of(gain, b), targets, group, capacity, tokens)


def gain_of(gain, block):
    return gain[0:1, block * LANES : (block + 1) * LANES]


def mix_rows(picks, base_of, weights, returned, blocks, group, capacity, tokens):
    count, rows = group * capacity, group * tokens
    given = [
        jnp.concatenate([part[number * count : (number + 1) * count, :] for part in returned], axis=0)
        for number in range(blocks // group)
    ]
    for number, picked in enumerate(side_by_side(picks, given)):
        total = base_of(number).astype(jnp.float32)
        for choice in range(TOP):
            total += weights[choice] * picked[choice * rows : (choice + 1) * rows, :]
        yield number, total.astype(jnp.bfloat16)


def relay_kernel(micro, partners, capacity, group, info, *refs):
    @pl.when(info[0] == 0)
    def _():
        relay_rows(micro, partners, capacity, group, info, *refs)


def relay_rows(micro, partners, capacity, group, info, tokens_ref, ids, weights, next_ids, next_gain, *rest):
    returned, outs, (state_to, *carry_to) = rest[:partners], rest[-partners - 5 : -6], rest[-partners - 8 : -partners - 5]
    given, arrived, state_out, carried, made, left = rest[-6:]
    own_to, kept_to = carry_to
    copy = pltpu.make_async_copy(tokens_ref.at[micro], given, arrived.at[0])
    copy.start()
    tokens, width = given.shape
    blocks = width // LANES
    state = carried.at[blocks * capacity : blocks * (capacity + tokens), :]
    picks = picks_to_mix(ids[0, micro] ^ info[1], partners, capacity, group)
    shares = spread_columns(weights[0, micro], group * tokens)
    total = jnp.zeros((tokens, 1), jnp.float32)
    copy.wait()

    def base_of(number):
        return jnp.concatenate(
            [given[:, b * LANES : (b + 1) * LANES] for b in range(number * group, (number + 1) * group)], axis=0
        )

    for number, mixed in mix_rows(picks, base_of, shares, returned, blocks, group, capacity, tokens):
        state[number * group * tokens : (number + 1) * group * tokens, :] = mixed
        wide = mixed.astype(jnp.float32)
        square = jnp.sum(wide * wide, axis=1, keepdims=True)
        for j in range(group):
            b = number * group + j
            state_out[:, b * LANES : (b + 1) * LANES] = mixed[j * tokens : (j + 1) * tokens, :]
            total += square[j * tokens : (j + 1) * tokens, :]
    scale = lax.rsqrt(total * (1.0 / width) + EPS)
    own = blocks * capacity
    copies = [pltpu.make_async_copy(state_out, state_to, left.at[0])]
    copies += [pltpu.make_async_copy(carried.at[pl.ds(own, state.shape[0])], kept_to, left.at[1])]
    for copy in copies:
        copy.start()
    targets = [carried] + [made.at[k] for k in range(partners - 1)]
    send_rows(
        next_ids[0, micro] ^ info[1], state, scale, lambda b: gain_of(next_gain, b), targets, group, capacity, tokens
    )
    sends = [pltpu.make_async_copy(made.at[k], outs[k], left.at[3 + k]) for k in range(partners - 1)]
    sends += [pltpu.make_async_copy(carried.at[pl.ds(0, own)], own_to, left.at[2])]
    for copy in sends:
        copy.start()
    for copy in copies + sends:
        copy.wait()


def last_kernel(micro, partners, capacity, group, info, first, carried, ids, weights, *rest):
    returned, (out, made, done) = rest[:partners], rest[-3:]
    tokens, width = made.shape
    blocks = width // LANES
    keep = pltpu.make_async_copy(made, out.at[0, micro], done.at[0])

    @pl.when(info[0] == 0)
    def _():
        copy = pltpu.make_async_copy(first, made, done.at[1])
        copy.start()
        copy.wait()

    @pl.when(info[0] != 0)
    def _():
        picks = picks_to_mix(ids[0, micro] ^ info[1], partners, capacity, group)
        shares = spread_columns(weights[0, micro], group * tokens)

        def base_of(number):
            return carried[number * group * tokens : (number + 1) * group * tokens, :]

        for number, mixed in mix_rows(picks, base_of, shares, returned, blocks, group, capacity, tokens):
            for j in range(group):
                b = number * group + j
                made[:, b * LANES : (b + 1) * LANES] = mixed[j * tokens : (j + 1) * tokens, :]

    keep.start()
    keep.wait()


def expert_kernel(section, partners, offsets, capacity, group, split, unroll, info, *refs):
    @pl.when(info[0] == section)
    def _():
        expert_rows(partners, offsets, capacity, group, split, unroll, *refs)


def expert_rows(partners, offsets, capacity, group, split, unroll, *refs):
    halves, first = [], 0
    for pieces in split:
        halves.append(refs[first : first + pieces])
        first += pieces
    sent, outs = refs[first : first + partners], refs[-10 - partners : -10]
    numbers, places, placed, weights, arrived, state, hidden, total, made, left = refs[-10:]
    blocks = state.shape[0]
    padded = state.shape[1] // partners
    columns = (weights.shape[1] - 1) // 3
    count = group * capacity
    sizes = [columns] * 3 + [1]

    def part_of(k, number):
        return sent[k][number * count : (number + 1) * count, :]

    def load(half, which):
        source, start = halves[half][0], which * columns
        if len(halves[half]) > 1:
            source, start = halves[half][min(which, 2)], columns if which == 3 else 0
        return pltpu.make_async_copy(
            source.at[pl.ds(start, sizes[which])],
            weights.at[half, pl.ds(which * columns, sizes[which])],
            arrived.at[half, which],
        )

    for which in (3,), (0, 1), (2,):
        for half in range(len(halves)):
            for piece in which:
                load(half, piece).start()

    shape = (group * padded, count)
    block, slot = split_by(iota((group * padded, 1), 0), padded)
    key = jnp.where(slot < capacity, block * capacity + slot, -1)
    spread = jnp.where(iota(shape, 1) == key, 1.0, 0.0).astype(jnp.bfloat16)
    for number in range(blocks // group):
        spaced = side_by_side(
            spread, [p[at + number * count : at + (number + 1) * count, :] for p, at in zip(sent, offsets)]
        )
        for j in range(group):
            rows = jnp.concatenate([s[j * padded : (j + 1) * padded, :] for s in spaced], axis=0)
            state[number * group + j] = rows.astype(jnp.bfloat16)
            total[number * group + j] = jnp.zeros(rows.shape, jnp.float32)

    for half in range(len(halves)):
        load(half, 3).wait()
        numbers[half] = weights[half, 3 * columns, :16, :].astype(jnp.float32)[:8, :].astype(jnp.int32)
    moves = [pltpu.make_async_copy(numbers.at[half], places.at[half], placed.at[half]) for half in range(len(halves))]
    for move in moves:
        move.start()
    for move in moves:
        move.wait()

    for half in range(len(halves)):
        load(half, 0).wait()
        load(half, 1).wait()

        def up_step(at, carry, half=half):
            for i in range(unroll):
                c = at * unroll + i
                rows = state[places[half, 0, c]]
                both = dot(rows, jnp.concatenate([weights[half, c], weights[half, columns + c]], axis=1))
                gate, up = both[:, :LANES], both[:, LANES:]
                hidden[half * columns + c] = (gate / (1.0 + jnp.exp(-gate)) * up).astype(jnp.bfloat16)
            return carry

        lax.fori_loop(0, columns // unroll, up_step, 0)

    for half in range(len(halves)):
        load(half, 2).wait()

        def down_step(at, carry, half=half):
            produced = []
            for i in range(unroll):
                c = at * unroll + i
                produced.append(dot(hidden[half * columns + c], weights[half, 2 * columns + c]))
            for i in range(unroll):
                to = places[half, 1, at * unroll + i]
                total[to] = total[to] + produced[i]
            return carry

        lax.fori_loop(0, columns // unroll, down_step, 0)

    block, slot = split_by(iota((count, 1), 0), capacity)
    packing = jnp.where(iota((count, group * padded), 1) == block * padded + slot, 1.0, 0.0).astype(jnp.bfloat16)
    copies = [pltpu.make_async_copy(made.at[k], outs[k], left.at[k]) for k in range(partners)]
    for number in range(blocks // group):
        spaced = [
            jnp.concatenate(
                [total[number * group + j, k * padded : (k + 1) * padded, :] for j in range(group)], axis=0
            ).astype(jnp.bfloat16)
            for k in range(partners)
        ]
        for k, rows in enumerate(side_by_side(packing, spaced)):
            made[k, number * count : (number + 1) * count, :] = rows.astype(jnp.bfloat16)
    for copy in copies:
        copy.start()
    for copy in copies:
        copy.wait()


def pack_kernel(info, in_rows, out_cols, *refs):
    stored, (out, kept, numbers, named, arrived, left) = refs[:3], refs[-6:]
    columns = stored[0].shape[0]
    names = [
        pltpu.make_async_copy(source, numbers.at[at], named.at[at]) for at, source in enumerate((in_rows, out_cols))
    ]

    def take(at):
        return pltpu.make_async_copy(stored[at], kept.at[pl.ds(at * columns, columns)], arrived.at[at])

    def give(at):
        span = pl.ds(at * columns, columns + at // 2)
        return pltpu.make_async_copy(kept.at[span], out.at[span], left.at[at])

    for name in names:
        name.start()
    for at in range(3):
        take(at).start()
    spread = jnp.where(iota((columns, LANES), 0) == iota((columns, LANES), 1), 1.0, 0.0).astype(jnp.bfloat16)
    row = iota((LANES, LANES), 0)
    for name in names:
        name.wait()
    rows, cols = (
        dot(jnp.broadcast_to(numbers[at].astype(jnp.float32), (LANES, columns)).astype(jnp.bfloat16), spread)
        for at in range(2)
    )
    kept[3 * columns] = jnp.where(row == 0, rows, jnp.where(row == 1, cols, 0.0)).astype(jnp.bfloat16)
    for at in range(3):
        take(at).wait()
        give(at).start()
    for at in range(3):
        give(at).wait()


def tie_kernel(*refs):
    pass


SMEM = pl.BlockSpec(memory_space=pltpu.SMEM)
VMEM = pl.BlockSpec(memory_space=pltpu.VMEM)
ANY = pl.BlockSpec(memory_space=pl.ANY)


def held(*arrays):
    return [pltpu.with_memory_space_constraint(a, pltpu.HBM) for a in arrays]


def pack(info, places, weights, after):
    columns, *block = weights[0].shape
    shape = (3 * columns + 1, *block)
    return pl.pallas_call(
        pack_kernel,
        out_shape=pltpu.HBM(shape, jnp.bfloat16),
        in_specs=[SMEM] + [ANY] * (5 + len(after)),
        out_specs=ANY,
        scratch_shapes=[
            pltpu.VMEM(shape, jnp.bfloat16),
            pltpu.VMEM((2, 1, columns), jnp.int32),
            pltpu.SemaphoreType.DMA((2,)),
            pltpu.SemaphoreType.DMA((3,)),
            pltpu.SemaphoreType.DMA((3,)),
        ],
        compiler_params=pltpu.CompilerParams(vmem_limit_bytes=8 * MIB),
        name="pack",
    )(info, *held(*places, *weights), *after)


def tie(array, *others):
    return pl.pallas_call(
        tie_kernel,
        out_shape=pltpu.HBM(array.shape, array.dtype),
        in_specs=[ANY] * (1 + len(others)),
        out_specs=ANY,
        input_output_aliases={0: 0},
        name="tie",
    )(*held(array), *others)


def body(tokens, norm_gain, route_ids, route_weights, gate_blocks, up_blocks, down_blocks, gate_rows, down_cols):
    partners = lax.axis_size("expert")
    sections = lax.axis_size("section")
    shards = lax.axis_size("shard")
    micro_count, row_count, width = tokens.shape
    assert sections == 2 and gate_blocks.shape[1] == 1 and partners & (partners - 1) == 0
    assert lax.axis_size("groups") == 2
    blocks = width // LANES
    capacity = min(row_count, max(row_count * 9 // 16, row_count * TOP // partners + 2))
    group = group_of(capacity)
    size = blocks * capacity
    padded = up_to(capacity, 8)
    bf16, f32 = jnp.bfloat16, jnp.float32
    rows_shape = jax.ShapeDtypeStruct((size, LANES), bf16)
    carry_rows = size + blocks * row_count
    carry_shapes = [pltpu.HBM((size, LANES), bf16), pltpu.HBM((carry_rows - size, LANES), bf16)]
    state_shape = jax.ShapeDtypeStruct((row_count, width), bf16)
    info = jnp.stack([lax.axis_index(a) for a in ("section", "expert")]).astype(jnp.int32)
    weights = [a.reshape(a.shape[2:3] + a.shape[4:]) for a in (gate_blocks, up_blocks, down_blocks)]
    places = [a.reshape(1, -1) for a in (gate_rows, down_cols)]
    ids, shares = jnp.swapaxes(route_ids, 2, 3), jnp.swapaxes(route_weights, 2, 3)
    axes = ("groups", "shard", "expert", "section")
    sizes = [lax.axis_size(a) for a in axes]

    def trade(array, *moves):
        pairs = []
        for place in itertools.product(*(range(n) for n in sizes)):
            if moves[place[3]]:
                target = moves[place[3]](*place)
                pairs.append(tuple(sum(p * math.prod(sizes[i + 1 :]) for i, p in enumerate(q)) for q in (place, target)))
        return lax.ppermute(array, axes, pairs)

    def idle(g, s, e, c):
        return g ^ 1, s, e, c

    def to_partner(k):
        return lambda g, s, e, c: (g, s, e ^ k, c)

    def to_next(k):
        return lambda g, s, e, c: (g, s, e ^ k, 1)

    def idle_back(g, s, e, c):
        return g ^ 1, s, e, 0

    def across(g, s, e, c):
        return g, s ^ 1, e, c

    def exchange(parts, *moves_of):
        moved = list(parts)
        for k in range(partners - 1, 0, -1):
            moved[k] = trade(parts[k], *(m(k) for m in moves_of))
        return moved

    def swap(array):
        return lax.ppermute(array, "section", [(0, 1), (1, 0)])

    def always(move):
        return lambda k: move

    paired = shards == 2
    if not paired:
        weights = [lax.all_gather(a, "shard", axis=0, tiled=True) for a in weights]
        places = [lax.all_gather(a, "shard", axis=1, tiled=True) for a in places]
    columns = weights[0].shape[0]
    assert columns <= LANES

    def call(kernel, name, out_shape, args, specs, scratch, limit, out_specs=None, aliases={}):
        return pl.pallas_call(
            kernel,
            out_shape=out_shape,
            in_specs=specs,
            out_specs=out_specs or [VMEM] * len(out_shape),
            scratch_shapes=scratch,
            input_output_aliases=aliases,
            compiler_params=pltpu.CompilerParams(vmem_limit_bytes=limit * MIB),
            name=name,
        )(*args)

    def expert(layer, sources, rows, offsets, after):
        return call(
            functools.partial(
                expert_kernel, layer, partners, offsets, capacity, group, [1] * len(sources), math.gcd(columns, 32)
            ),
            "expert",
            [pltpu.HBM(rows_shape.shape, bf16)] * partners,
            (info, *held(*sources), *rows, *after),
            [SMEM] + [ANY] * len(sources) + [VMEM] * partners + [ANY] * len(after),
            [
                pltpu.VMEM((len(sources), 8, LANES), jnp.int32),
                pltpu.SMEM((len(sources), 8, LANES), jnp.int32),
                pltpu.SemaphoreType.DMA((len(sources),)),
                pltpu.VMEM((len(sources), 3 * columns + 1) + weights[0].shape[1:], bf16),
                pltpu.SemaphoreType.DMA((len(sources), 4)),
                pltpu.VMEM((blocks, partners * padded, LANES), bf16),
                pltpu.VMEM((len(sources) * columns, partners * padded, LANES), bf16),
                pltpu.VMEM((blocks, partners * padded, LANES), f32),
                pltpu.VMEM((partners,) + rows_shape.shape, bf16),
                pltpu.SemaphoreType.DMA((partners,)),
            ],
            22,
            [ANY] * partners,
        )

    packed = pack(info, places, weights, [])
    next_ids, next_gain = swap(ids), swap(norm_gain)
    sent = call(
        functools.partial(first_send_kernel, partners, capacity, group),
        "first_send",
        [jax.ShapeDtypeStruct((micro_count * size, LANES), bf16)] * partners,
        (info, *held(tokens), ids, norm_gain, next_ids, next_gain),
        [SMEM, ANY, VMEM, VMEM, ANY, ANY],
        [
            pltpu.VMEM(tokens.shape, bf16),
            pltpu.VMEM((blocks * row_count, LANES), bf16),
            pltpu.SemaphoreType.DMA((1,)),
        ],
        16,
    )
    rows = exchange(sent, to_partner, always(None))
    sources = [[packed], [packed]]
    if paired:
        moved = tie(trade(packed, across, idle), *rows[1:])
        packed = tie(packed, moved)
        arrived = trade(packed, None, across)
        sources = [[packed, moved], [packed, arrived]]
    after = []
    back = []
    for micro in range(micro_count):
        done = expert(0, sources[0], rows, [micro * size] * partners, after)
        after = held(done[0])
        back.append(exchange(done, to_partner, always(idle)))
    firsts, carries, given_rows = [], [], []
    for micro in range(micro_count):
        first, *sent = call(
            functools.partial(relay_kernel, micro, partners, capacity, group),
            "relay",
            [pltpu.HBM(state_shape.shape, bf16), *carry_shapes] + [pltpu.HBM(rows_shape.shape, bf16)] * (partners - 1),
            (info, *held(tokens), ids, shares, next_ids, next_gain, *held(back[micro][0]), *back[micro][1:], *after),
            [SMEM, ANY] + [VMEM] * (4 + partners) + [ANY] * len(after),
            [
                pltpu.VMEM((row_count, width), bf16),
                pltpu.SemaphoreType.DMA((1,)),
                pltpu.VMEM((row_count, width), bf16),
                pltpu.VMEM((carry_rows, LANES), bf16),
                pltpu.VMEM((partners - 1,) + rows_shape.shape, bf16),
                pltpu.SemaphoreType.DMA((partners + 2,)),
            ],
            12,
            [ANY] * (partners + 2),
        )
        after = held(first)
        firsts.append(first)
        carries.append(sent[: 1 - partners])
        given_rows.append(exchange([None] + sent[1 - partners :], to_next, always(idle_back)))
    carries[0][0] = swap(carries[0][0])
    after = held(first)
    back = []
    for micro in range(micro_count):
        if micro:
            carries[micro][0] = swap(tie(carries[micro][0], done[0]))
        done = expert(1, sources[1], [carries[micro][0]] + given_rows[micro][1:], [0] * partners, after)
        after = []
        carries[micro][1] = swap(tie(carries[micro][1], done[0]))
        back.append(exchange(done, always(idle), to_partner))
    out = None
    for micro in range(micro_count):
        kept = [] if out is None else held(out)
        out = call(
            functools.partial(last_kernel, micro, partners, capacity, group),
            "last",
            pltpu.HBM((1, micro_count, row_count, width), bf16),
            (
                info,
                *held(firsts[micro]),
                carries[micro][1],
                ids,
                shares,
                *held(back[micro][0]),
                *back[micro][1:],
                *kept,
            ),
            [SMEM, ANY] + [VMEM] * (3 + partners) + [ANY] * len(kept),
            [pltpu.VMEM((row_count, width), bf16), pltpu.SemaphoreType.DMA((2,))],
            12,
            ANY,
            {5 + partners: 0} if kept else {},
        )
    return out


def solution(mesh):
    in_specs = (
        P(None, ("groups", "shard", "expert"), None),
        P("section", None),
        P("section", None, ("groups", "shard", "expert"), None),
        P("section", None, ("groups", "shard", "expert"), None),
        P("section", "expert", "shard", None, None, None),
        P("section", "expert", "shard", None, None, None),
        P("section", "expert", "shard", None, None, None),
        P("section", "expert", "shard", None),
        P("section", "expert", "shard", None),
    )
    out_specs = P("section", None, ("groups", "shard", "expert"), None)
    return jax.shard_map(body, mesh=mesh, in_specs=in_specs, out_specs=out_specs, check_vma=False)
```

```python
import functools
import itertools
import math

import jax
import jax.numpy as jnp
from jax import lax
from jax.experimental import pallas as pl
from jax.experimental.pallas import tpu as pltpu
from jax.sharding import PartitionSpec as P

TOP = 2
LANES = 128
EPS = 1e-05
MIB = 1 << 20


def up_to(value, unit):
    return -(-value // unit) * unit


def group_of(capacity):
    return 16 // math.gcd(capacity, 16)


def iota(shape, axis):
    return lax.broadcasted_iota(jnp.int32, shape, axis)


def split_by(values, unit):
    quotient = jnp.floor((values.astype(jnp.float32) + 0.5) * (1.0 / unit)).astype(jnp.int32)
    return quotient, values - quotient * unit


def dot(left, right, contract=((1,), (0,))):
    return lax.dot_general(left, right, (contract, ((), ())), preferred_element_type=jnp.float32)


def side_by_side(left, rights):
    products = []
    for at in range(0, len(rights), 2):
        pair = rights[at : at + 2]
        product = dot(left, jnp.concatenate(pair, axis=1))
        products += [product[:, i * LANES : (i + 1) * LANES] for i in range(len(pair))]
    return products


def spread_columns(values, rows):
    tokens = values.shape[1]
    token = split_by(iota((rows, tokens), 0), tokens)[1]
    same = iota((rows, tokens), 1) == token
    return [
        jnp.sum(jnp.where(same, values[choice : choice + 1, :], 0.0), axis=1, keepdims=True) for choice in range(TOP)
    ]


def picks_to_send(ids, experts, capacity, group):
    tokens = ids.shape[1]
    expert = iota((up_to(experts, 16), tokens), 0)
    hit = (ids[0:1, :] == expert) | (ids[1:2, :] == expert)
    hit = jnp.where(hit, 1.0, 0.0).astype(jnp.bfloat16)
    shape = (tokens, group * tokens)
    block, token = split_by(iota(shape, 1), tokens)
    earlier = jnp.where(iota(shape, 0) < token, 1.0, 0.0).astype(jnp.bfloat16)
    same = jnp.where(iota(shape, 0) == token, 1.0, 0.0).astype(jnp.bfloat16)
    slot = dot(hit, earlier)
    here = dot(hit, same)
    first = (block[0:1, :] * capacity).astype(jnp.float32)
    key = jnp.where(here > 0.5, slot + first, -1.0)
    row = iota((group * capacity, group * tokens), 0).astype(jnp.float32)
    return jnp.concatenate(
        [jnp.where(row == key[k : k + 1, :], 1.0, 0.0) for k in range(experts)], axis=0
    ).astype(jnp.bfloat16)


def picks_to_mix(ids, experts, capacity, group):
    tokens = ids.shape[1]
    rows = group * tokens
    token = split_by(iota((rows, tokens), 0), tokens)[1]
    first = (split_by(iota((rows, 1), 0), tokens)[0] * capacity).astype(jnp.float32)
    columns = iota((rows, experts * group * capacity), 1).astype(jnp.float32)
    earlier = iota((rows, tokens), 1) < token
    chosen = spread_columns(ids.astype(jnp.float32), rows)
    parts = []
    for choice in range(TOP):
        expert = chosen[choice]
        named = (ids[0:1, :].astype(jnp.float32) == expert) | (ids[1:2, :].astype(jnp.float32) == expert)
        slot = jnp.sum(jnp.where(named & earlier, 1.0, 0.0), axis=1, keepdims=True)
        key = expert * (group * capacity) + first + slot
        parts.append(jnp.where(columns == key, 1.0, 0.0))
    return jnp.concatenate(parts, axis=0).astype(jnp.bfloat16)


def send_rows(partners, state, scale, gain_of, outs, group, capacity, tokens):
    count = group * capacity
    blocks = state.shape[0] // tokens
    picks = picks_to_send(partners, len(outs), capacity, group)
    scale = jnp.concatenate([scale] * group, axis=0)
    normed = []
    for number in range(blocks // group):
        rows = state[number * group * tokens : (number + 1) * group * tokens, :]
        gain = jnp.concatenate(
            [jnp.broadcast_to(gain_of(number * group + j), (tokens, LANES)) for j in range(group)], axis=0
        )
        normed.append((rows.astype(jnp.float32) * scale * gain).astype(jnp.bfloat16))
    for number, picked in enumerate(side_by_side(picks, normed)):
        for k, out in enumerate(outs):
            out[number * count : (number + 1) * count, :] = picked[k * count : (k + 1) * count, :].astype(jnp.bfloat16)


def first_send_kernel(partners, capacity, group, info, tokens_ref, ids, gain, *rest):
    outs, (given, state, arrived) = rest[-partners - 3 : -3], rest[-3:]

    @pl.when(info[0] == 0)
    def _():
        copy = pltpu.make_async_copy(tokens_ref, given, arrived.at[0])
        copy.start()
        copy.wait()
        micro_count, tokens, width = given.shape
        blocks = width // LANES
        for micro in range(micro_count):
            total = jnp.zeros((tokens, 1), jnp.float32)
            for b in range(blocks):
                part = given[micro, :, b * LANES : (b + 1) * LANES]
                state[b * tokens : (b + 1) * tokens, :] = part
                wide = part.astype(jnp.float32)
                total += jnp.sum(wide * wide, axis=1, keepdims=True)
            scale = lax.rsqrt(total * (1.0 / width) + EPS)
            size = blocks * capacity
            targets = [out.at[micro * size : (micro + 1) * size, :] for out in outs]
            send_rows(ids[0, micro] ^ info[1], state, scale, lambda b: gain_of(gain, b), targets, group, capacity, tokens)


def gain_of(gain, block):
    return gain[0:1, block * LANES : (block + 1) * LANES]


def mix_rows(picks, base_of, weights, returned, blocks, group, capacity, tokens):
    count, rows = group * capacity, group * tokens
    given = [
        jnp.concatenate([part[number * count : (number + 1) * count, :] for part in returned], axis=0)
        for number in range(blocks // group)
    ]
    for number, picked in enumerate(side_by_side(picks, given)):
        total = base_of(number).astype(jnp.float32)
        for choice in range(TOP):
            total += weights[choice] * picked[choice * rows : (choice + 1) * rows, :]
        yield number, total.astype(jnp.bfloat16)


def relay_kernel(micro, partners, capacity, group, info, *refs):
    @pl.when(info[0] == 0)
    def _():
        relay_rows(micro, partners, capacity, group, info, *refs)


def relay_rows(micro, partners, capacity, group, info, tokens_ref, ids, weights, next_ids, next_gain, *rest):
    returned, outs, (state_to, *carry_to) = rest[:partners], rest[-partners - 5 : -6], rest[-partners - 8 : -partners - 5]
    given, arrived, state_out, carried, made, left = rest[-6:]
    own_to, kept_to = carry_to
    copy = pltpu.make_async_copy(tokens_ref.at[micro], given, arrived.at[0])
    copy.start()
    tokens, width = given.shape
    blocks = width // LANES
    state = carried.at[blocks * capacity : blocks * (capacity + tokens), :]
    picks = picks_to_mix(ids[0, micro] ^ info[1], partners, capacity, group)
    shares = spread_columns(weights[0, micro], group * tokens)
    total = jnp.zeros((tokens, 1), jnp.float32)
    copy.wait()

    def base_of(number):
        return jnp.concatenate(
            [given[:, b * LANES : (b + 1) * LANES] for b in range(number * group, (number + 1) * group)], axis=0
        )

    for number, mixed in mix_rows(picks, base_of, shares, returned, blocks, group, capacity, tokens):
        state[number * group * tokens : (number + 1) * group * tokens, :] = mixed
        wide = mixed.astype(jnp.float32)
        square = jnp.sum(wide * wide, axis=1, keepdims=True)
        for j in range(group):
            b = number * group + j
            state_out[:, b * LANES : (b + 1) * LANES] = mixed[j * tokens : (j + 1) * tokens, :]
            total += square[j * tokens : (j + 1) * tokens, :]
    scale = lax.rsqrt(total * (1.0 / width) + EPS)
    own = blocks * capacity
    copies = [pltpu.make_async_copy(state_out, state_to, left.at[0])]
    copies += [pltpu.make_async_copy(carried.at[pl.ds(own, state.shape[0])], kept_to, left.at[1])]
    for copy in copies:
        copy.start()
    targets = [carried] + [made.at[k] for k in range(partners - 1)]
    send_rows(
        next_ids[0, micro] ^ info[1], state, scale, lambda b: gain_of(next_gain, b), targets, group, capacity, tokens
    )
    sends = [pltpu.make_async_copy(made.at[k], outs[k], left.at[3 + k]) for k in range(partners - 1)]
    sends += [pltpu.make_async_copy(carried.at[pl.ds(0, own)], own_to, left.at[2])]
    for copy in sends:
        copy.start()
    for copy in copies + sends:
        copy.wait()


def last_kernel(micro, partners, capacity, group, info, first, carried, ids, weights, *rest):
    returned, (out, made, done) = rest[:partners], rest[-3:]
    tokens, width = made.shape
    blocks = width // LANES
    keep = pltpu.make_async_copy(made, out.at[0, micro], done.at[0])

    @pl.when(info[0] == 0)
    def _():
        copy = pltpu.make_async_copy(first, made, done.at[1])
        copy.start()
        copy.wait()

    @pl.when(info[0] != 0)
    def _():
        picks = picks_to_mix(ids[0, micro] ^ info[1], partners, capacity, group)
        shares = spread_columns(weights[0, micro], group * tokens)

        def base_of(number):
            return carried[number * group * tokens : (number + 1) * group * tokens, :]

        for number, mixed in mix_rows(picks, base_of, shares, returned, blocks, group, capacity, tokens):
            for j in range(group):
                b = number * group + j
                made[:, b * LANES : (b + 1) * LANES] = mixed[j * tokens : (j + 1) * tokens, :]

    keep.start()
    keep.wait()


def expert_kernel(section, partners, offsets, capacity, group, split, unroll, info, *refs):
    @pl.when(info[0] == section)
    def _():
        expert_rows(partners, offsets, capacity, group, split, unroll, *refs)


def expert_rows(partners, offsets, capacity, group, split, unroll, *refs):
    halves, first = [], 0
    for pieces in split:
        halves.append(refs[first : first + pieces])
        first += pieces
    sent, outs = refs[first : first + partners], refs[-10 - partners : -10]
    numbers, places, placed, weights, arrived, state, hidden, total, made, left = refs[-10:]
    blocks = state.shape[0]
    padded = state.shape[1] // partners
    columns = (weights.shape[1] - 1) // 3
    count = group * capacity
    sizes = [columns] * 3 + [1]

    def part_of(k, number):
        return sent[k][number * count : (number + 1) * count, :]

    def load(half, which):
        source, start = halves[half][0], which * columns
        if len(halves[half]) > 1:
            source, start = halves[half][min(which, 2)], columns if which == 3 else 0
        return pltpu.make_async_copy(
            source.at[pl.ds(start, sizes[which])],
            weights.at[half, pl.ds(which * columns, sizes[which])],
            arrived.at[half, which],
        )

    for which in (3,), (0, 1), (2,):
        for half in range(len(halves)):
            for piece in which:
                load(half, piece).start()

    shape = (group * padded, count)
    block, slot = split_by(iota((group * padded, 1), 0), padded)
    key = jnp.where(slot < capacity, block * capacity + slot, -1)
    spread = jnp.where(iota(shape, 1) == key, 1.0, 0.0).astype(jnp.bfloat16)
    for number in range(blocks // group):
        spaced = side_by_side(
            spread, [p[at + number * count : at + (number + 1) * count, :] for p, at in zip(sent, offsets)]
        )
        for j in range(group):
            rows = jnp.concatenate([s[j * padded : (j + 1) * padded, :] for s in spaced], axis=0)
            state[number * group + j] = rows.astype(jnp.bfloat16)
            total[number * group + j] = jnp.zeros(rows.shape, jnp.float32)

    for half in range(len(halves)):
        load(half, 3).wait()
        numbers[half] = weights[half, 3 * columns, :16, :].astype(jnp.float32)[:8, :].astype(jnp.int32)
    moves = [pltpu.make_async_copy(numbers.at[half], places.at[half], placed.at[half]) for half in range(len(halves))]
    for move in moves:
        move.start()
    for move in moves:
        move.wait()

    for half in range(len(halves)):
        load(half, 0).wait()
        load(half, 1).wait()

        def up_step(at, carry, half=half):
            for i in range(unroll):
                c = at * unroll + i
                rows = state[places[half, 0, c]]
                both = dot(rows, jnp.concatenate([weights[half, c], weights[half, columns + c]], axis=1))
                gate, up = both[:, :LANES], both[:, LANES:]
                hidden[half * columns + c] = (gate / (1.0 + jnp.exp(-gate)) * up).astype(jnp.bfloat16)
            return carry

        lax.fori_loop(0, columns // unroll, up_step, 0)

    for half in range(len(halves)):
        load(half, 2).wait()

        def down_step(at, carry, half=half):
            produced = []
            for i in range(unroll):
                c = at * unroll + i
                produced.append(dot(hidden[half * columns + c], weights[half, 2 * columns + c]))
            for i in range(unroll):
                to = places[half, 1, at * unroll + i]
                total[to] = total[to] + produced[i]
            return carry

        lax.fori_loop(0, columns // unroll, down_step, 0)

    block, slot = split_by(iota((count, 1), 0), capacity)
    packing = jnp.where(iota((count, group * padded), 1) == block * padded + slot, 1.0, 0.0).astype(jnp.bfloat16)
    copies = [pltpu.make_async_copy(made.at[k], outs[k], left.at[k]) for k in range(partners)]
    for number in range(blocks // group):
        spaced = [
            jnp.concatenate(
                [total[number * group + j, k * padded : (k + 1) * padded, :] for j in range(group)], axis=0
            ).astype(jnp.bfloat16)
            for k in range(partners)
        ]
        for k, rows in enumerate(side_by_side(packing, spaced)):
            made[k, number * count : (number + 1) * count, :] = rows.astype(jnp.bfloat16)
    for copy in copies:
        copy.start()
    for copy in copies:
        copy.wait()


def pack_kernel(info, in_rows, out_cols, *refs):
    stored, (out, kept, numbers, named, arrived, left) = refs[:3], refs[-6:]
    columns = stored[0].shape[0]
    names = [
        pltpu.make_async_copy(source, numbers.at[at], named.at[at]) for at, source in enumerate((in_rows, out_cols))
    ]

    def take(at):
        return pltpu.make_async_copy(stored[at], kept.at[pl.ds(at * columns, columns)], arrived.at[at])

    def give(at):
        span = pl.ds(at * columns, columns + at // 2)
        return pltpu.make_async_copy(kept.at[span], out.at[span], left.at[at])

    for name in names:
        name.start()
    for at in range(3):
        take(at).start()
    for at in range(2):
        take(at).wait()
        give(at).start()
    spread = jnp.where(iota((columns, LANES), 0) == iota((columns, LANES), 1), 1.0, 0.0).astype(jnp.bfloat16)
    row = iota((LANES, LANES), 0)
    for name in names:
        name.wait()
    rows, cols = (
        dot(jnp.broadcast_to(numbers[at].astype(jnp.float32), (LANES, columns)).astype(jnp.bfloat16), spread)
        for at in range(2)
    )
    kept[3 * columns] = jnp.where(row == 0, rows, jnp.where(row == 1, cols, 0.0)).astype(jnp.bfloat16)
    take(2).wait()
    give(2).start()
    for at in range(3):
        give(at).wait()


def tie_kernel(*refs):
    pass


SMEM = pl.BlockSpec(memory_space=pltpu.SMEM)
VMEM = pl.BlockSpec(memory_space=pltpu.VMEM)
ANY = pl.BlockSpec(memory_space=pl.ANY)


def held(*arrays):
    return [pltpu.with_memory_space_constraint(a, pltpu.HBM) for a in arrays]


def pack(info, places, weights, after):
    columns, *block = weights[0].shape
    shape = (3 * columns + 1, *block)
    return pl.pallas_call(
        pack_kernel,
        out_shape=pltpu.HBM(shape, jnp.bfloat16),
        in_specs=[SMEM] + [ANY] * (5 + len(after)),
        out_specs=ANY,
        scratch_shapes=[
            pltpu.VMEM(shape, jnp.bfloat16),
            pltpu.VMEM((2, 1, columns), jnp.int32),
            pltpu.SemaphoreType.DMA((2,)),
            pltpu.SemaphoreType.DMA((3,)),
            pltpu.SemaphoreType.DMA((3,)),
        ],
        compiler_params=pltpu.CompilerParams(vmem_limit_bytes=8 * MIB),
        name="pack",
    )(info, *held(*places, *weights), *after)


def tie(array, *others):
    return pl.pallas_call(
        tie_kernel,
        out_shape=pltpu.HBM(array.shape, array.dtype),
        in_specs=[ANY] * (1 + len(others)),
        out_specs=ANY,
        input_output_aliases={0: 0},
        name="tie",
    )(*held(array), *others)


def body(tokens, norm_gain, route_ids, route_weights, gate_blocks, up_blocks, down_blocks, gate_rows, down_cols):
    partners = lax.axis_size("expert")
    sections = lax.axis_size("section")
    shards = lax.axis_size("shard")
    micro_count, row_count, width = tokens.shape
    assert sections == 2 and gate_blocks.shape[1] == 1 and partners & (partners - 1) == 0
    assert lax.axis_size("groups") == 2
    blocks = width // LANES
    capacity = min(row_count, max(row_count * 9 // 16, row_count * TOP // partners + 2))
    group = group_of(capacity)
    size = blocks * capacity
    padded = up_to(capacity, 8)
    bf16, f32 = jnp.bfloat16, jnp.float32
    rows_shape = jax.ShapeDtypeStruct((size, LANES), bf16)
    carry_rows = size + blocks * row_count
    carry_shapes = [pltpu.HBM((size, LANES), bf16), pltpu.HBM((carry_rows - size, LANES), bf16)]
    state_shape = jax.ShapeDtypeStruct((row_count, width), bf16)
    info = jnp.stack([lax.axis_index(a) for a in ("section", "expert")]).astype(jnp.int32)
    weights = [a.reshape(a.shape[2:3] + a.shape[4:]) for a in (gate_blocks, up_blocks, down_blocks)]
    places = [a.reshape(1, -1) for a in (gate_rows, down_cols)]
    ids, shares = jnp.swapaxes(route_ids, 2, 3), jnp.swapaxes(route_weights, 2, 3)
    axes = ("groups", "shard", "expert", "section")
    sizes = [lax.axis_size(a) for a in axes]

    def trade(array, *moves):
        pairs = []
        for place in itertools.product(*(range(n) for n in sizes)):
            if moves[place[3]]:
                target = moves[place[3]](*place)
                pairs.append(tuple(sum(p * math.prod(sizes[i + 1 :]) for i, p in enumerate(q)) for q in (place, target)))
        return lax.ppermute(array, axes, pairs)

    def idle(g, s, e, c):
        return g ^ 1, s, e, c

    def to_partner(k):
        return lambda g, s, e, c: (g, s, e ^ k, c)

    def to_next(k):
        return lambda g, s, e, c: (g, s, e ^ k, 1)

    def idle_back(g, s, e, c):
        return g ^ 1, s, e, 0

    def across(g, s, e, c):
        return g, s ^ 1, e, c

    def exchange(parts, *moves_of):
        moved = list(parts)
        for k in range(partners - 1, 0, -1):
            moved[k] = trade(parts[k], *(m(k) for m in moves_of))
        return moved

    def swap(array):
        return lax.ppermute(array, "section", [(0, 1), (1, 0)])

    def always(move):
        return lambda k: move

    paired = shards == 2
    if not paired:
        weights = [lax.all_gather(a, "shard", axis=0, tiled=True) for a in weights]
        places = [lax.all_gather(a, "shard", axis=1, tiled=True) for a in places]
    columns = weights[0].shape[0]
    assert columns <= LANES

    def call(kernel, name, out_shape, args, specs, scratch, limit, out_specs=None, aliases={}):
        return pl.pallas_call(
            kernel,
            out_shape=out_shape,
            in_specs=specs,
            out_specs=out_specs or [VMEM] * len(out_shape),
            scratch_shapes=scratch,
            input_output_aliases=aliases,
            compiler_params=pltpu.CompilerParams(vmem_limit_bytes=limit * MIB),
            name=name,
        )(*args)

    def expert(layer, sources, rows, offsets, after):
        return call(
            functools.partial(
                expert_kernel, layer, partners, offsets, capacity, group, [1] * len(sources), math.gcd(columns, 32)
            ),
            "expert",
            [pltpu.HBM(rows_shape.shape, bf16)] * partners,
            (info, *held(*sources), *rows, *after),
            [SMEM] + [ANY] * len(sources) + [VMEM] * partners + [ANY] * len(after),
            [
                pltpu.VMEM((len(sources), 8, LANES), jnp.int32),
                pltpu.SMEM((len(sources), 8, LANES), jnp.int32),
                pltpu.SemaphoreType.DMA((len(sources),)),
                pltpu.VMEM((len(sources), 3 * columns + 1) + weights[0].shape[1:], bf16),
                pltpu.SemaphoreType.DMA((len(sources), 4)),
                pltpu.VMEM((blocks, partners * padded, LANES), bf16),
                pltpu.VMEM((len(sources) * columns, partners * padded, LANES), bf16),
                pltpu.VMEM((blocks, partners * padded, LANES), f32),
                pltpu.VMEM((partners,) + rows_shape.shape, bf16),
                pltpu.SemaphoreType.DMA((partners,)),
            ],
            22,
            [ANY] * partners,
        )

    packed = pack(info, places, weights, [])
    next_ids, next_gain = swap(ids), swap(norm_gain)
    sent = call(
        functools.partial(first_send_kernel, partners, capacity, group),
        "first_send",
        [jax.ShapeDtypeStruct((micro_count * size, LANES), bf16)] * partners,
        (info, *held(tokens), ids, norm_gain, next_ids, next_gain),
        [SMEM, ANY, VMEM, VMEM, ANY, ANY],
        [
            pltpu.VMEM(tokens.shape, bf16),
            pltpu.VMEM((blocks * row_count, LANES), bf16),
            pltpu.SemaphoreType.DMA((1,)),
        ],
        16,
    )
    rows = exchange(sent, to_partner, always(None))
    sources = [[packed], [packed]]
    if paired:
        moved = tie(trade(packed, across, idle), *rows[1:])
        packed = tie(packed, moved)
        arrived = trade(packed, None, across)
        sources = [[packed, moved], [packed, arrived]]
    after = []
    back = []
    for micro in range(micro_count):
        done = expert(0, sources[0], rows, [micro * size] * partners, after)
        after = held(done[0])
        back.append(exchange(done, to_partner, always(idle)))
    firsts, carries, given_rows = [], [], []
    for micro in range(micro_count):
        first, *sent = call(
            functools.partial(relay_kernel, micro, partners, capacity, group),
            "relay",
            [pltpu.HBM(state_shape.shape, bf16), *carry_shapes] + [pltpu.HBM(rows_shape.shape, bf16)] * (partners - 1),
            (info, *held(tokens), ids, shares, next_ids, next_gain, *held(back[micro][0]), *back[micro][1:], *after),
            [SMEM, ANY] + [VMEM] * (4 + partners) + [ANY] * len(after),
            [
                pltpu.VMEM((row_count, width), bf16),
                pltpu.SemaphoreType.DMA((1,)),
                pltpu.VMEM((row_count, width), bf16),
                pltpu.VMEM((carry_rows, LANES), bf16),
                pltpu.VMEM((partners - 1,) + rows_shape.shape, bf16),
                pltpu.SemaphoreType.DMA((partners + 2,)),
            ],
            12,
            [ANY] * (partners + 2),
        )
        after = held(first)
        firsts.append(first)
        carries.append(sent[: 1 - partners])
        given_rows.append(exchange([None] + sent[1 - partners :], to_next, always(idle_back)))
    carries[0][0] = swap(carries[0][0])
    after = held(first)
    back = []
    for micro in range(micro_count):
        if micro:
            carries[micro][0] = swap(tie(carries[micro][0], done[0]))
        done = expert(1, sources[1], [carries[micro][0]] + given_rows[micro][1:], [0] * partners, after)
        after = []
        carries[micro][1] = swap(tie(carries[micro][1], done[0]))
        back.append(exchange(done, always(idle), to_partner))
    out = None
    for micro in range(micro_count):
        kept = [] if out is None else held(out)
        out = call(
            functools.partial(last_kernel, micro, partners, capacity, group),
            "last",
            pltpu.HBM((1, micro_count, row_count, width), bf16),
            (
                info,
                *held(firsts[micro]),
                carries[micro][1],
                ids,
                shares,
                *held(back[micro][0]),
                *back[micro][1:],
                *kept,
            ),
            [SMEM, ANY] + [VMEM] * (3 + partners) + [ANY] * len(kept),
            [pltpu.VMEM((row_count, width), bf16), pltpu.SemaphoreType.DMA((2,))],
            12,
            ANY,
            {5 + partners: 0} if kept else {},
        )
    return out


def solution(mesh):
    in_specs = (
        P(None, ("groups", "shard", "expert"), None),
        P("section", None),
        P("section", None, ("groups", "shard", "expert"), None),
        P("section", None, ("groups", "shard", "expert"), None),
        P("section", "expert", "shard", None, None, None),
        P("section", "expert", "shard", None, None, None),
        P("section", "expert", "shard", None, None, None),
        P("section", "expert", "shard", None),
        P("section", "expert", "shard", None),
    )
    out_specs = P("section", None, ("groups", "shard", "expert"), None)
    return jax.shard_map(body, mesh=mesh, in_specs=in_specs, out_specs=out_specs, check_vma=False)
```

```python
import functools
import itertools
import math

import jax
import jax.numpy as jnp
from jax import lax
from jax.experimental import pallas as pl
from jax.experimental.pallas import tpu as pltpu
from jax.sharding import PartitionSpec as P

TOP = 2
LANES = 128
EPS = 1e-05
MIB = 1 << 20


def up_to(value, unit):
    return -(-value // unit) * unit


def group_of(capacity):
    return 16 // math.gcd(capacity, 16)


def iota(shape, axis):
    return lax.broadcasted_iota(jnp.int32, shape, axis)


def split_by(values, unit):
    quotient = jnp.floor((values.astype(jnp.float32) + 0.5) * (1.0 / unit)).astype(jnp.int32)
    return quotient, values - quotient * unit


def dot(left, right, contract=((1,), (0,))):
    return lax.dot_general(left, right, (contract, ((), ())), preferred_element_type=jnp.float32)


def side_by_side(left, rights):
    products = []
    for at in range(0, len(rights), 2):
        pair = rights[at : at + 2]
        product = dot(left, jnp.concatenate(pair, axis=1))
        products += [product[:, i * LANES : (i + 1) * LANES] for i in range(len(pair))]
    return products


def spread_columns(values, rows):
    tokens = values.shape[1]
    token = split_by(iota((rows, tokens), 0), tokens)[1]
    same = iota((rows, tokens), 1) == token
    return [
        jnp.sum(jnp.where(same, values[choice : choice + 1, :], 0.0), axis=1, keepdims=True) for choice in range(TOP)
    ]


def picks_to_send(ids, experts, capacity, group):
    tokens = ids.shape[1]
    expert = iota((up_to(experts, 16), tokens), 0)
    hit = (ids[0:1, :] == expert) | (ids[1:2, :] == expert)
    hit = jnp.where(hit, 1.0, 0.0).astype(jnp.bfloat16)
    shape = (tokens, group * tokens)
    block, token = split_by(iota(shape, 1), tokens)
    earlier = jnp.where(iota(shape, 0) < token, 1.0, 0.0).astype(jnp.bfloat16)
    same = jnp.where(iota(shape, 0) == token, 1.0, 0.0).astype(jnp.bfloat16)
    slot = dot(hit, earlier)
    here = dot(hit, same)
    first = (block[0:1, :] * capacity).astype(jnp.float32)
    key = jnp.where(here > 0.5, slot + first, -1.0)
    row = iota((group * capacity, group * tokens), 0).astype(jnp.float32)
    return jnp.concatenate(
        [jnp.where(row == key[k : k + 1, :], 1.0, 0.0) for k in range(experts)], axis=0
    ).astype(jnp.bfloat16)


def picks_to_mix(ids, experts, capacity, group):
    tokens = ids.shape[1]
    rows = group * tokens
    token = split_by(iota((rows, tokens), 0), tokens)[1]
    first = (split_by(iota((rows, 1), 0), tokens)[0] * capacity).astype(jnp.float32)
    columns = iota((rows, experts * group * capacity), 1).astype(jnp.float32)
    earlier = iota((rows, tokens), 1) < token
    chosen = spread_columns(ids.astype(jnp.float32), rows)
    parts = []
    for choice in range(TOP):
        expert = chosen[choice]
        named = (ids[0:1, :].astype(jnp.float32) == expert) | (ids[1:2, :].astype(jnp.float32) == expert)
        slot = jnp.sum(jnp.where(named & earlier, 1.0, 0.0), axis=1, keepdims=True)
        key = expert * (group * capacity) + first + slot
        parts.append(jnp.where(columns == key, 1.0, 0.0))
    return jnp.concatenate(parts, axis=0).astype(jnp.bfloat16)


def send_rows(partners, state, scale, gain_of, outs, group, capacity, tokens):
    count = group * capacity
    blocks = state.shape[0] // tokens
    picks = picks_to_send(partners, len(outs), capacity, group)
    scale = jnp.concatenate([scale] * group, axis=0)
    normed = []
    for number in range(blocks // group):
        rows = state[number * group * tokens : (number + 1) * group * tokens, :]
        gain = jnp.concatenate(
            [jnp.broadcast_to(gain_of(number * group + j), (tokens, LANES)) for j in range(group)], axis=0
        )
        normed.append((rows.astype(jnp.float32) * scale * gain).astype(jnp.bfloat16))
    for number, picked in enumerate(side_by_side(picks, normed)):
        for k, out in enumerate(outs):
            out[number * count : (number + 1) * count, :] = picked[k * count : (k + 1) * count, :].astype(jnp.bfloat16)


def first_send_kernel(partners, capacity, group, info, tokens_ref, ids, gain, *rest):
    outs, (given, state, arrived) = rest[-partners - 3 : -3], rest[-3:]

    @pl.when(info[0] == 0)
    def _():
        copy = pltpu.make_async_copy(tokens_ref, given, arrived.at[0])
        copy.start()
        copy.wait()
        micro_count, tokens, width = given.shape
        blocks = width // LANES
        for micro in range(micro_count):
            total = jnp.zeros((tokens, 1), jnp.float32)
            for b in range(blocks):
                part = given[micro, :, b * LANES : (b + 1) * LANES]
                state[b * tokens : (b + 1) * tokens, :] = part
                wide = part.astype(jnp.float32)
                total += jnp.sum(wide * wide, axis=1, keepdims=True)
            scale = lax.rsqrt(total * (1.0 / width) + EPS)
            size = blocks * capacity
            targets = [out.at[micro * size : (micro + 1) * size, :] for out in outs]
            send_rows(ids[0, micro] ^ info[1], state, scale, lambda b: gain_of(gain, b), targets, group, capacity, tokens)


def gain_of(gain, block):
    return gain[0:1, block * LANES : (block + 1) * LANES]


def mix_rows(picks, base_of, weights, returned, blocks, group, capacity, tokens):
    count, rows = group * capacity, group * tokens
    given = [
        jnp.concatenate([part[number * count : (number + 1) * count, :] for part in returned], axis=0)
        for number in range(blocks // group)
    ]
    for number, picked in enumerate(side_by_side(picks, given)):
        total = base_of(number).astype(jnp.float32)
        for choice in range(TOP):
            total += weights[choice] * picked[choice * rows : (choice + 1) * rows, :]
        yield number, total.astype(jnp.bfloat16)


def relay_kernel(micro, partners, capacity, group, info, *refs):
    @pl.when(info[0] == 0)
    def _():
        relay_rows(micro, partners, capacity, group, info, *refs)


def relay_rows(micro, partners, capacity, group, info, tokens_ref, ids, weights, next_ids, next_gain, *rest):
    returned, outs, (state_to, *carry_to) = rest[:partners], rest[-partners - 5 : -6], rest[-partners - 8 : -partners - 5]
    given, arrived, state_out, carried, made, left = rest[-6:]
    own_to, kept_to = carry_to
    copy = pltpu.make_async_copy(tokens_ref.at[micro], given, arrived.at[0])
    copy.start()
    tokens, width = given.shape
    blocks = width // LANES
    state = carried.at[blocks * capacity : blocks * (capacity + tokens), :]
    picks = picks_to_mix(ids[0, micro] ^ info[1], partners, capacity, group)
    shares = spread_columns(weights[0, micro], group * tokens)
    total = jnp.zeros((tokens, 1), jnp.float32)
    copy.wait()

    def base_of(number):
        return jnp.concatenate(
            [given[:, b * LANES : (b + 1) * LANES] for b in range(number * group, (number + 1) * group)], axis=0
        )

    for number, mixed in mix_rows(picks, base_of, shares, returned, blocks, group, capacity, tokens):
        state[number * group * tokens : (number + 1) * group * tokens, :] = mixed
        wide = mixed.astype(jnp.float32)
        square = jnp.sum(wide * wide, axis=1, keepdims=True)
        for j in range(group):
            b = number * group + j
            state_out[:, b * LANES : (b + 1) * LANES] = mixed[j * tokens : (j + 1) * tokens, :]
            total += square[j * tokens : (j + 1) * tokens, :]
    scale = lax.rsqrt(total * (1.0 / width) + EPS)
    own = blocks * capacity
    copies = [pltpu.make_async_copy(state_out, state_to, left.at[0])]
    copies += [pltpu.make_async_copy(carried.at[pl.ds(own, state.shape[0])], kept_to, left.at[1])]
    for copy in copies:
        copy.start()
    targets = [carried] + [made.at[k] for k in range(partners - 1)]
    send_rows(
        next_ids[0, micro] ^ info[1], state, scale, lambda b: gain_of(next_gain, b), targets, group, capacity, tokens
    )
    sends = [pltpu.make_async_copy(made.at[k], outs[k], left.at[3 + k]) for k in range(partners - 1)]
    sends += [pltpu.make_async_copy(carried.at[pl.ds(0, own)], own_to, left.at[2])]
    for copy in sends:
        copy.start()
    for copy in copies + sends:
        copy.wait()


def last_kernel(micro, partners, capacity, group, info, first, carried, ids, weights, *rest):
    returned, (out, made, done) = rest[:partners], rest[-3:]
    tokens, width = made.shape
    blocks = width // LANES
    cut = blocks // group // 2 * group * LANES
    spans = pl.ds(0, cut), pl.ds(cut, width - cut)
    keeps = [pltpu.make_async_copy(made.at[:, p], out.at[0, micro, :, p], done.at[i]) for i, p in enumerate(spans)]

    @pl.when(info[0] == 0)
    def _():
        copy = pltpu.make_async_copy(first, made, done.at[1])
        copy.start()
        copy.wait()
        keeps[0].start()

    @pl.when(info[0] != 0)
    def _():
        picks = picks_to_mix(ids[0, micro] ^ info[1], partners, capacity, group)
        shares = spread_columns(weights[0, micro], group * tokens)

        def base_of(number):
            return carried[number * group * tokens : (number + 1) * group * tokens, :]

        for number, mixed in mix_rows(picks, base_of, shares, returned, blocks, group, capacity, tokens):
            for j in range(group):
                b = number * group + j
                made[:, b * LANES : (b + 1) * LANES] = mixed[j * tokens : (j + 1) * tokens, :]
            if (number + 1) * group * LANES == cut:
                keeps[0].start()

    keeps[1].start()
    for keep in keeps:
        keep.wait()


def expert_kernel(section, partners, offsets, capacity, group, split, unroll, info, *refs):
    @pl.when(info[0] == section)
    def _():
        expert_rows(partners, offsets, capacity, group, split, unroll, *refs)


def expert_rows(partners, offsets, capacity, group, split, unroll, *refs):
    halves, first = [], 0
    for pieces in split:
        halves.append(refs[first : first + pieces])
        first += pieces
    sent, outs = refs[first : first + partners], refs[-10 - partners : -10]
    numbers, places, placed, weights, arrived, state, hidden, total, made, left = refs[-10:]
    blocks = state.shape[0]
    padded = state.shape[1] // partners
    columns = (weights.shape[1] - 1) // 3
    count = group * capacity
    sizes = [columns] * 3 + [1]

    def part_of(k, number):
        return sent[k][number * count : (number + 1) * count, :]

    def load(half, which):
        source, start = halves[half][0], which * columns
        if len(halves[half]) > 1:
            source, start = halves[half][min(which, 2)], columns if which == 3 else 0
        return pltpu.make_async_copy(
            source.at[pl.ds(start, sizes[which])],
            weights.at[half, pl.ds(which * columns, sizes[which])],
            arrived.at[half, which],
        )

    for which in (3,), (0, 1), (2,):
        for half in range(len(halves)):
            for piece in which:
                load(half, piece).start()

    shape = (group * padded, count)
    block, slot = split_by(iota((group * padded, 1), 0), padded)
    key = jnp.where(slot < capacity, block * capacity + slot, -1)
    spread = jnp.where(iota(shape, 1) == key, 1.0, 0.0).astype(jnp.bfloat16)
    for number in range(blocks // group):
        spaced = side_by_side(
            spread, [p[at + number * count : at + (number + 1) * count, :] for p, at in zip(sent, offsets)]
        )
        for j in range(group):
            rows = jnp.concatenate([s[j * padded : (j + 1) * padded, :] for s in spaced], axis=0)
            state[number * group + j] = rows.astype(jnp.bfloat16)
            total[number * group + j] = jnp.zeros(rows.shape, jnp.float32)

    for half in range(len(halves)):
        load(half, 3).wait()
        numbers[half] = weights[half, 3 * columns, :16, :].astype(jnp.float32)[:8, :].astype(jnp.int32)
    moves = [pltpu.make_async_copy(numbers.at[half], places.at[half], placed.at[half]) for half in range(len(halves))]
    for move in moves:
        move.start()
    for move in moves:
        move.wait()

    for half in range(len(halves)):
        load(half, 0).wait()
        load(half, 1).wait()

        def up_step(at, carry, half=half):
            for i in range(unroll):
                c = at * unroll + i
                rows = state[places[half, 0, c]]
                both = dot(rows, jnp.concatenate([weights[half, c], weights[half, columns + c]], axis=1))
                gate, up = both[:, :LANES], both[:, LANES:]
                hidden[half * columns + c] = (gate / (1.0 + jnp.exp(-gate)) * up).astype(jnp.bfloat16)
            return carry

        lax.fori_loop(0, columns // unroll, up_step, 0)

    for half in range(len(halves)):
        load(half, 2).wait()

        def down_step(at, carry, half=half):
            produced = []
            for i in range(unroll):
                c = at * unroll + i
                produced.append(dot(hidden[half * columns + c], weights[half, 2 * columns + c]))
            for i in range(unroll):
                to = places[half, 1, at * unroll + i]
                total[to] = total[to] + produced[i]
            return carry

        lax.fori_loop(0, columns // unroll, down_step, 0)

    block, slot = split_by(iota((count, 1), 0), capacity)
    packing = jnp.where(iota((count, group * padded), 1) == block * padded + slot, 1.0, 0.0).astype(jnp.bfloat16)
    copies = [pltpu.make_async_copy(made.at[k], outs[k], left.at[k]) for k in range(partners)]
    for number in range(blocks // group):
        spaced = [
            jnp.concatenate(
                [total[number * group + j, k * padded : (k + 1) * padded, :] for j in range(group)], axis=0
            ).astype(jnp.bfloat16)
            for k in range(partners)
        ]
        for k, rows in enumerate(side_by_side(packing, spaced)):
            made[k, number * count : (number + 1) * count, :] = rows.astype(jnp.bfloat16)
    for copy in copies:
        copy.start()
    for copy in copies:
        copy.wait()


def pack_kernel(info, in_rows, out_cols, *refs):
    stored, (out, kept, numbers, named, arrived, left) = refs[:3], refs[-6:]
    columns = stored[0].shape[0]
    names = [
        pltpu.make_async_copy(source, numbers.at[at], named.at[at]) for at, source in enumerate((in_rows, out_cols))
    ]

    def take(at):
        return pltpu.make_async_copy(stored[at], kept.at[pl.ds(at * columns, columns)], arrived.at[at])

    def give(at):
        span = pl.ds(at * columns, columns + at // 2)
        return pltpu.make_async_copy(kept.at[span], out.at[span], left.at[at])

    for name in names:
        name.start()
    for at in range(3):
        take(at).start()
    for at in range(2):
        take(at).wait()
        give(at).start()
    spread = jnp.where(iota((columns, LANES), 0) == iota((columns, LANES), 1), 1.0, 0.0).astype(jnp.bfloat16)
    row = iota((LANES, LANES), 0)
    for name in names:
        name.wait()
    rows, cols = (
        dot(jnp.broadcast_to(numbers[at].astype(jnp.float32), (LANES, columns)).astype(jnp.bfloat16), spread)
        for at in range(2)
    )
    kept[3 * columns] = jnp.where(row == 0, rows, jnp.where(row == 1, cols, 0.0)).astype(jnp.bfloat16)
    take(2).wait()
    give(2).start()
    for at in range(3):
        give(at).wait()


def tie_kernel(*refs):
    pass


SMEM = pl.BlockSpec(memory_space=pltpu.SMEM)
VMEM = pl.BlockSpec(memory_space=pltpu.VMEM)
ANY = pl.BlockSpec(memory_space=pl.ANY)


def held(*arrays):
    return [pltpu.with_memory_space_constraint(a, pltpu.HBM) for a in arrays]


def pack(info, places, weights, after):
    columns, *block = weights[0].shape
    shape = (3 * columns + 1, *block)
    return pl.pallas_call(
        pack_kernel,
        out_shape=pltpu.HBM(shape, jnp.bfloat16),
        in_specs=[SMEM] + [ANY] * (5 + len(after)),
        out_specs=ANY,
        scratch_shapes=[
            pltpu.VMEM(shape, jnp.bfloat16),
            pltpu.VMEM((2, 1, columns), jnp.int32),
            pltpu.SemaphoreType.DMA((2,)),
            pltpu.SemaphoreType.DMA((3,)),
            pltpu.SemaphoreType.DMA((3,)),
        ],
        compiler_params=pltpu.CompilerParams(vmem_limit_bytes=8 * MIB),
        name="pack",
    )(info, *held(*places, *weights), *after)


def tie(array, *others):
    return pl.pallas_call(
        tie_kernel,
        out_shape=pltpu.HBM(array.shape, array.dtype),
        in_specs=[ANY] * (1 + len(others)),
        out_specs=ANY,
        input_output_aliases={0: 0},
        name="tie",
    )(*held(array), *others)


def body(tokens, norm_gain, route_ids, route_weights, gate_blocks, up_blocks, down_blocks, gate_rows, down_cols):
    partners = lax.axis_size("expert")
    sections = lax.axis_size("section")
    shards = lax.axis_size("shard")
    micro_count, row_count, width = tokens.shape
    assert sections == 2 and gate_blocks.shape[1] == 1 and partners & (partners - 1) == 0
    assert lax.axis_size("groups") == 2
    blocks = width // LANES
    capacity = min(row_count, max(row_count * 9 // 16, row_count * TOP // partners + 2))
    group = group_of(capacity)
    size = blocks * capacity
    padded = up_to(capacity, 8)
    bf16, f32 = jnp.bfloat16, jnp.float32
    rows_shape = jax.ShapeDtypeStruct((size, LANES), bf16)
    carry_rows = size + blocks * row_count
    carry_shapes = [pltpu.HBM((size, LANES), bf16), pltpu.HBM((carry_rows - size, LANES), bf16)]
    state_shape = jax.ShapeDtypeStruct((row_count, width), bf16)
    info = jnp.stack([lax.axis_index(a) for a in ("section", "expert")]).astype(jnp.int32)
    weights = [a.reshape(a.shape[2:3] + a.shape[4:]) for a in (gate_blocks, up_blocks, down_blocks)]
    places = [a.reshape(1, -1) for a in (gate_rows, down_cols)]
    ids, shares = jnp.swapaxes(route_ids, 2, 3), jnp.swapaxes(route_weights, 2, 3)
    axes = ("groups", "shard", "expert", "section")
    sizes = [lax.axis_size(a) for a in axes]

    def trade(array, *moves):
        pairs = []
        for place in itertools.product(*(range(n) for n in sizes)):
            if moves[place[3]]:
                target = moves[place[3]](*place)
                pairs.append(tuple(sum(p * math.prod(sizes[i + 1 :]) for i, p in enumerate(q)) for q in (place, target)))
        return lax.ppermute(array, axes, pairs)

    def idle(g, s, e, c):
        return g ^ 1, s, e, c

    def to_partner(k):
        return lambda g, s, e, c: (g, s, e ^ k, c)

    def to_next(k):
        return lambda g, s, e, c: (g, s, e ^ k, 1)

    def idle_back(g, s, e, c):
        return g ^ 1, s, e, 0

    def across(g, s, e, c):
        return g, s ^ 1, e, c

    def exchange(parts, *moves_of):
        moved = list(parts)
        for k in range(partners - 1, 0, -1):
            moved[k] = trade(parts[k], *(m(k) for m in moves_of))
        return moved

    def swap(array):
        return lax.ppermute(array, "section", [(0, 1), (1, 0)])

    def always(move):
        return lambda k: move

    paired = shards == 2
    if not paired:
        weights = [lax.all_gather(a, "shard", axis=0, tiled=True) for a in weights]
        places = [lax.all_gather(a, "shard", axis=1, tiled=True) for a in places]
    columns = weights[0].shape[0]
    assert columns <= LANES

    def call(kernel, name, out_shape, args, specs, scratch, limit, out_specs=None, aliases={}):
        return pl.pallas_call(
            kernel,
            out_shape=out_shape,
            in_specs=specs,
            out_specs=out_specs or [VMEM] * len(out_shape),
            scratch_shapes=scratch,
            input_output_aliases=aliases,
            compiler_params=pltpu.CompilerParams(vmem_limit_bytes=limit * MIB),
            name=name,
        )(*args)

    def expert(layer, sources, rows, offsets, after):
        return call(
            functools.partial(
                expert_kernel, layer, partners, offsets, capacity, group, [1] * len(sources), math.gcd(columns, 32)
            ),
            "expert",
            [pltpu.HBM(rows_shape.shape, bf16)] * partners,
            (info, *held(*sources), *rows, *after),
            [SMEM] + [ANY] * len(sources) + [VMEM] * partners + [ANY] * len(after),
            [
                pltpu.VMEM((len(sources), 8, LANES), jnp.int32),
                pltpu.SMEM((len(sources), 8, LANES), jnp.int32),
                pltpu.SemaphoreType.DMA((len(sources),)),
                pltpu.VMEM((len(sources), 3 * columns + 1) + weights[0].shape[1:], bf16),
                pltpu.SemaphoreType.DMA((len(sources), 4)),
                pltpu.VMEM((blocks, partners * padded, LANES), bf16),
                pltpu.VMEM((len(sources) * columns, partners * padded, LANES), bf16),
                pltpu.VMEM((blocks, partners * padded, LANES), f32),
                pltpu.VMEM((partners,) + rows_shape.shape, bf16),
                pltpu.SemaphoreType.DMA((partners,)),
            ],
            22,
            [ANY] * partners,
        )

    packed = pack(info, places, weights, [])
    next_ids, next_gain = swap(ids), swap(norm_gain)
    sent = call(
        functools.partial(first_send_kernel, partners, capacity, group),
        "first_send",
        [jax.ShapeDtypeStruct((micro_count * size, LANES), bf16)] * partners,
        (info, *held(tokens), ids, norm_gain, next_ids, next_gain),
        [SMEM, ANY, VMEM, VMEM, ANY, ANY],
        [
            pltpu.VMEM(tokens.shape, bf16),
            pltpu.VMEM((blocks * row_count, LANES), bf16),
            pltpu.SemaphoreType.DMA((1,)),
        ],
        16,
    )
    rows = exchange(sent, to_partner, always(None))
    sources = [[packed], [packed]]
    if paired:
        moved = tie(trade(packed, across, idle), *rows[1:])
        packed = tie(packed, moved)
        arrived = trade(packed, None, across)
        sources = [[packed, moved], [packed, arrived]]
    after = []
    back = []
    for micro in range(micro_count):
        done = expert(0, sources[0], rows, [micro * size] * partners, after)
        after = held(done[0])
        back.append(exchange(done, to_partner, always(idle)))
    firsts, carries, given_rows = [], [], []
    for micro in range(micro_count):
        first, *sent = call(
            functools.partial(relay_kernel, micro, partners, capacity, group),
            "relay",
            [pltpu.HBM(state_shape.shape, bf16), *carry_shapes] + [pltpu.HBM(rows_shape.shape, bf16)] * (partners - 1),
            (info, *held(tokens), ids, shares, next_ids, next_gain, *held(back[micro][0]), *back[micro][1:], *after),
            [SMEM, ANY] + [VMEM] * (4 + partners) + [ANY] * len(after),
            [
                pltpu.VMEM((row_count, width), bf16),
                pltpu.SemaphoreType.DMA((1,)),
                pltpu.VMEM((row_count, width), bf16),
                pltpu.VMEM((carry_rows, LANES), bf16),
                pltpu.VMEM((partners - 1,) + rows_shape.shape, bf16),
                pltpu.SemaphoreType.DMA((partners + 2,)),
            ],
            12,
            [ANY] * (partners + 2),
        )
        after = held(first)
        firsts.append(first)
        carries.append(sent[: 1 - partners])
        given_rows.append(exchange([None] + sent[1 - partners :], to_next, always(idle_back)))
    carries[0][0] = swap(carries[0][0])
    after = held(first)
    back = []
    for micro in range(micro_count):
        if micro:
            carries[micro][0] = swap(tie(carries[micro][0], done[0]))
        done = expert(1, sources[1], [carries[micro][0]] + given_rows[micro][1:], [0] * partners, after)
        after = []
        carries[micro][1] = swap(tie(carries[micro][1], done[0]))
        back.append(exchange(done, always(idle), to_partner))
    out = None
    for micro in range(micro_count):
        kept = [] if out is None else held(out)
        out = call(
            functools.partial(last_kernel, micro, partners, capacity, group),
            "last",
            pltpu.HBM((1, micro_count, row_count, width), bf16),
            (
                info,
                *held(firsts[micro]),
                carries[micro][1],
                ids,
                shares,
                *held(back[micro][0]),
                *back[micro][1:],
                *kept,
            ),
            [SMEM, ANY] + [VMEM] * (3 + partners) + [ANY] * len(kept),
            [pltpu.VMEM((row_count, width), bf16), pltpu.SemaphoreType.DMA((2,))],
            12,
            ANY,
            {5 + partners: 0} if kept else {},
        )
    return out


def solution(mesh):
    in_specs = (
        P(None, ("groups", "shard", "expert"), None),
        P("section", None),
        P("section", None, ("groups", "shard", "expert"), None),
        P("section", None, ("groups", "shard", "expert"), None),
        P("section", "expert", "shard", None, None, None),
        P("section", "expert", "shard", None, None, None),
        P("section", "expert", "shard", None, None, None),
        P("section", "expert", "shard", None),
        P("section", "expert", "shard", None),
    )
    out_specs = P("section", None, ("groups", "shard", "expert"), None)
    return jax.shard_map(body, mesh=mesh, in_specs=in_specs, out_specs=out_specs, check_vma=False)
```
